1024 devices in a mesh: dp: 16 (over y, x_lo), expert: 32 (over z, x_hi), fsdp: 2 (over core).
Axes of the slice: x: 8 (x_hi: 4, x_lo: 2; x = x_hi * 2 + x_lo), y: 8, z: 8, core: 2. Of those that a mesh axis runs over, the one named last changes fastest.
Arguments:
- cotangent: bfloat16 [65536, 2880], P(('dp', 'expert'), 'fsdp'), may hold values from -6 to 6
- route_weight: bfloat16 [65536, 4], P(('dp', 'expert')), may hold values from 0.099609375 to 0.8984375
- expert_ids: int32 [65536, 4], P(('dp', 'expert')), may hold values from 0 to 31, all different within a row; in each aligned block of 128 rows (0 to 127, 128 to 255, ...) at most 20 rows name the same one
- down_weight: bfloat16 [32, 1536, 2880], P('expert', 'fsdp'), may hold values from -0.15625 to 0.15625
- hidden_act: bfloat16 [16, 32, 32, 20, 1536], P('dp', 'expert', None, None, 'fsdp'), may hold values from -0.1875 to 0.1875
Outputs:
- hidden_grad: bfloat16 [16, 32, 32, 20, 1536], P('dp', 'expert', None, None, 'fsdp')
- route_grad: float32 [65536, 4], P(('dp', 'expert'))
The draws below stay inside these ranges and needn't reach their ends.
Inputs may be any that keep to these rules, and one draw needn't show every extreme that they name: `expert_ids`: among the 128 rows of one block each expert is named at most 20 times, and in every draw some expert is named exactly 20 times by the rows of some block; the 4 experts of a row differ.
All inputs are finite; a program needn't handle non-finite values.
Results may differ from the reference program's by a relative error of at most 0.0065.
Values may be sent and summed in bfloat16 or wider, within the bound.
No kernel may reach another device: no remote copies, remote signals or barrier semaphores. Data moves between devices by JAX's collectives and lax.ppermute only.
A program may use at most 128 MiB of HBM per device.

```python
import math
import jax
import jax.numpy as jnp
import numpy as np
from jax import lax

D = 2880
HID = 1536
TOPK = 4
TOK_DEV = 128
EXPERTS = 32
CAP = 20
TOKENS = 65536
N_DP = 16
N_EXPERT = 32


def shard_levels(own_key, extent, cuts, smallest, largest):
    factor_of, own = 1.0, jax.random.fold_in(own_key, 6)
    for dim, blocks in cuts:
        heights = jnp.exp(jax.random.uniform(jax.random.fold_in(own, dim), (blocks,), jnp.float32, smallest / len(cuts), largest / len(cuts)))
        factor_of = factor_of * jnp.repeat(heights, extent[dim] // blocks).reshape([-1 if axis == dim else 1 for axis in range(len(extent))])
    return factor_of


def deal_out(key, own, number, rows, amount, top, most, slope):
    order = jax.random.permutation(key, amount)
    heavy_load, ordinary = load_shares(amount, rows * top, most, slope, True), load_shares(amount, rows * top, most, slope, False)
    places = jnp.arange(amount)

    def named(lengths, offset_by):
        used = int((lengths > 0).sum())
        fixed = max(1, used // 4)
        passed = fixed + (places - fixed + offset_by * (used - fixed)) % max(1, amount - fixed)
        return jnp.zeros((amount,), jnp.int32).at[order[jnp.where(places < fixed, places, passed)]].set(jnp.asarray(lengths, jnp.int32))

    lengths = jnp.where(number % 4 == 0, named(heavy_load, number // 4), named(ordinary, number - number // 4 - 1))
    mixed = jax.random.permutation(jax.random.fold_in(own, 3), amount)
    donor, taker = mixed[0:amount // 2 * 2:2], mixed[1:amount // 2 * 2:2]
    margin = jnp.minimum(lengths[donor] - 1, most - lengths[taker]) // 2
    margin = jnp.where((donor == order[0]) | (taker == order[0]) | (lengths[taker] == 0), 0, jnp.maximum(margin, 0))
    passed = jax.random.randint(jax.random.fold_in(own, 4), (amount // 2,), 0, 1 << 20) % (margin + 1)
    lengths = lengths.at[donor].add(-passed).at[taker].add(passed)
    members = jnp.searchsorted(jnp.cumsum(lengths), jnp.arange(rows * top), side="right").astype(jnp.int32)
    listing = members.reshape(top, rows).T
    listing = listing[jax.random.permutation(jax.random.fold_in(own, 1), rows)]
    offset_by = jax.random.randint(jax.random.fold_in(own, 2), (rows, 1), 0, top)
    return jnp.take_along_axis(listing, (jnp.arange(top)[None, :] + offset_by) % top, axis=1)


def load_shares(count, total, reach, lean, full):
    portions = [(1 << 20) // math.isqrt(rank ** lean) + 1 for rank in range(1, count + 1)]
    largest = reach if full else min(reach, max(-(-total // count), total * portions[0] // sum(portions)))
    least = 1 if total - largest >= count - 1 else 0
    counts, rest = [largest] + [least] * (count - 1), total - largest - least * (count - 1)
    while rest > 0:
        candidates = [i for i in range(1, count) if counts[i] < largest] or [i for i in range(1, count) if counts[i] < reach]
        mass, budget = sum([portions[i] for i in candidates]), rest
        for i in candidates:
            extra = min(reach - counts[i], max(1, budget * portions[i] // mass), rest)
            counts[i] = counts[i] + extra
            rest = rest - extra
    return np.array(counts)


def scatter_about(own_key, shape, deviation, most, shards=(), kind=jnp.bfloat16):
    level = shard_levels(own_key, shape, shards, -0.22, 0.18) if shards else 1.0
    result = jax.random.normal(own_key, shape, jnp.float32) * deviation * level
    return jnp.minimum(jnp.maximum(result, -most), most).astype(kind)


def setup_inputs(seed: int = 0) -> dict:
    arg_keys = jax.random.split(jax.random.key(seed), 6)
    cotangent = scatter_about(arg_keys[0], (TOKENS, D), 1.0, 6.0, ((0, 512), (1, 2)))
    route_weight = jnp.clip(0.099609375 + 0.7988281 * jax.random.uniform(arg_keys[1], (TOKENS, TOPK), jnp.float32) ** shard_levels(arg_keys[1], (TOKENS, TOPK), ((0, 512),), -0.2, 0.2), 0.099609375, 0.8984375).astype(jnp.bfloat16)
    expert_ids_keys = jax.random.split(jax.random.fold_in(arg_keys[2], 1), TOKENS // TOK_DEV)
    expert_ids_turns = jax.random.permutation(jax.random.fold_in(arg_keys[2], 3), TOKENS // TOK_DEV)
    expert_ids = jax.vmap(lambda own, number: deal_out(jax.random.fold_in(arg_keys[2], 2), own, number, TOK_DEV, EXPERTS, TOPK, CAP, 2))(expert_ids_keys, expert_ids_turns).reshape((TOKENS, TOPK))
    down_weight = scatter_about(arg_keys[3], (EXPERTS, HID, D), HID ** -0.5, 0.15625, ((0, 32), (1, 2)))
    hidden_act = scatter_about(arg_keys[4], (N_DP, EXPERTS, N_EXPERT, CAP, HID), 0.03, 0.1875, ((0, 16), (1, 32), (4, 2)))
    return {"cotangent": cotangent, "route_weight": route_weight, "expert_ids": expert_ids, "down_weight": down_weight, "hidden_act": hidden_act}


def slot_table(expert_ids):
    flat = expert_ids.reshape(-1)
    choices_hit = (flat[:, None] == jnp.arange(EXPERTS, dtype=jnp.int32)[None, :]).astype(jnp.int32)
    earlier = jnp.cumsum(choices_hit, axis=0) - choices_hit
    slots = jnp.sum(earlier * choices_hit, axis=1).reshape(expert_ids.shape)
    hit_expert = expert_ids[:, :, None] == jnp.arange(EXPERTS, dtype=jnp.int32)[None, None, :]
    hit_slot = slots[:, :, None] == jnp.arange(CAP, dtype=jnp.int32)[None, None, :]
    return (hit_expert[:, :, :, None] & hit_slot[:, :, None, :]).astype(jnp.float32)


def reference(cotangent, route_weight, expert_ids, down_weight, hidden_act):
    cot_all = cotangent.reshape(N_DP, N_EXPERT, TOK_DEV, D)
    weight_all = route_weight.reshape(N_DP, N_EXPERT, TOK_DEV, TOPK)
    ids_all = expert_ids.reshape(N_DP, N_EXPERT, TOK_DEV, TOPK)

    def one_group(group_args):
        cot_group, weight_group, ids_group, act_group = group_args
        selector = jax.vmap(slot_table)(ids_group)
        filled = jnp.sum(selector, axis=(1, 2))
        positions = jnp.arange(TOK_DEV, dtype=jnp.float32)
        token_index = jnp.einsum("atkes,t->aes", selector, positions).astype(jnp.int32)
        picked = jax.vmap(lambda block, where: block[where])(cot_group, token_index)
        picked = jnp.where(filled[..., None] > 0.5, picked, jnp.zeros_like(picked))
        slot_rows = jnp.transpose(picked, (1, 0, 2, 3))
        slot_weights = jnp.einsum("atkes,atk->eas", selector, weight_group.astype(jnp.float32))

        def one_expert(expert_args):
            rows_e, weights_e, matrix_e, act_e = expert_args
            projected = jnp.dot(rows_e.reshape(-1, D), matrix_e.T, preferred_element_type=jnp.float32)
            projected = projected.reshape(N_EXPERT, CAP, HID)
            grad_e = (weights_e[..., None] * projected).astype(jnp.bfloat16)
            dots_e = jnp.sum(act_e.astype(jnp.float32) * projected, axis=-1)
            return grad_e, dots_e

        grad_group, dots_group = lax.map(one_expert, (slot_rows, slot_weights, down_weight, act_group))
        route_group = jnp.einsum("atkes,eas->atk", selector, dots_group)
        return grad_group, route_group

    hidden_grad, route_grad = lax.map(one_group, (cot_all, weight_all, ids_all, hidden_act))
    return hidden_grad, route_grad.reshape(TOKENS, TOPK)
```

```python
import jax
import jax.numpy as jnp
from jax import lax
from jax.experimental import pallas as pl
from jax.experimental.pallas import tpu as pltpu
from jax.sharding import PartitionSpec as P

LANES = 128
SUB = 8
FULL = 16
F32 = jnp.float32
BF16 = jnp.bfloat16
NT = (((1,), (1,)), ((), ()))
NN = (((1,), (0,)), ((), ()))


def ranks(ids, experts):
    topk, tokens = ids.shape
    expert = lax.broadcasted_iota(jnp.int32, (experts, tokens), 0)
    hit = jnp.zeros((experts, tokens), F32)
    for k in range(topk):
        hit = hit + (ids[k : k + 1, :] == expert).astype(F32)
    earlier = lax.broadcasted_iota(jnp.int32, (tokens, tokens), 0) < lax.broadcasted_iota(
        jnp.int32, (tokens, tokens), 1
    )
    before = lax.dot_general(
        hit.astype(BF16), earlier.astype(F32).astype(BF16), NN, preferred_element_type=F32
    )
    return jnp.where(hit > 0.5, before, -1.0)


def pack_kernel(ids_ref, weight_ref, cot_ref, send_ref, rank_ref):
    experts = send_ref.shape[0]
    width, tokens = cot_ref.shape
    blocks = -(-width // LANES)
    half = blocks // 2
    whole = width // LANES * LANES
    ids = ids_ref[...]
    rank = ranks(ids, experts)
    rank_ref[...] = rank
    expert = lax.broadcasted_iota(jnp.int32, (experts, tokens), 0)
    gate = jnp.zeros((experts, tokens), F32)
    for k in range(ids.shape[0]):
        gate = gate + jnp.where(
            ids[k : k + 1, :] == expert, weight_ref[k : k + 1, :].astype(F32), 0.0
        )

    cot = cot_ref[...]
    tail = jnp.concatenate(
        [cot[whole:], jnp.zeros((LANES - (width - whole), tokens), BF16)], axis=0
    )
    free = (
        lax.broadcasted_iota(jnp.int32, (LANES, tokens), 0) >= width - whole
    ).astype(F32).astype(BF16)

    def pick(rows, columns):
        return lax.dot_general(rows, columns, NT, preferred_element_type=F32)

    def put(first, count, value):
        send_ref[:, first : first + count, :] = value.astype(BF16).reshape(experts, count, LANES)

    def select(count, wanted):
        rows = lax.broadcasted_iota(jnp.int32, (experts, count, tokens), 1)
        chosen = (rank[:, None, :] == wanted(rows).astype(F32)).astype(F32)
        gated = chosen * gate[:, None, :]
        return (
            chosen.reshape(experts * count, tokens).astype(BF16),
            gated.reshape(experts * count, tokens).astype(BF16),
        )

    rows_a, gated_a = select(FULL, lambda r: r)
    for b in range(blocks - 1):
        put(b * FULL, FULL, pick(rows_a, cot[b * LANES : (b + 1) * LANES]))
    put((blocks - 1) * FULL, FULL, pick(rows_a, tail) + pick(gated_a, free))

    base = blocks * FULL
    rows_l, _ = select(SUB, lambda r: jnp.where(r < SUB // 2, r + FULL, -2))
    rows_h, gated_h = select(SUB, lambda r: jnp.where(r < SUB // 2, -2, r + FULL - SUB // 2))
    for b in range(half):
        low = pick(rows_l, cot[b * LANES : (b + 1) * LANES])
        if half + b < blocks - 1:
            high = pick(rows_h, cot[(half + b) * LANES : (half + b + 1) * LANES])
        else:
            high = pick(rows_h, tail) + pick(gated_h, free)
        put(base + b * SUB, SUB, low + high)


def project_kernel(
    core_ref, own_ref, other_ref, weight_ref, act_ref, grad_ref, dots_ref, part_a, part_b, gate_a, gate_b
):
    sources = own_ref.shape[0]
    depth, hidden = weight_ref.shape
    width = depth // 2
    blocks = -(-width // LANES)
    half = blocks // 2
    whole = width // LANES * LANES
    tail = width - whole
    base = blocks * FULL
    columns = hidden // LANES
    core = core_ref[0]
    mine = core * width
    theirs = width - mine

    def block(ref, first, count):
        return ref[:, first : first + count, :].reshape(sources * count, LANES)

    def weight(first, count):
        return [
            weight_ref[pl.ds(pl.multiple_of(start + first, 16), count), :] for start in (mine, theirs)
        ]

    def mm(rows, columns_):
        return lax.dot_general(
            jnp.concatenate(rows, axis=1),
            jnp.concatenate(columns_, axis=0),
            NN,
            preferred_element_type=F32,
        )

    refs = (own_ref, other_ref)
    tail_w = weight(whole, tail)
    full_a = [[block(ref, b * FULL, FULL) for b in range(blocks - 1)] for ref in refs]
    ends_a = [block(ref, (blocks - 1) * FULL, FULL) for ref in refs]
    out_a = mm(full_a[0] + full_a[1], weight(0, whole)) + mm([x[:, :tail] for x in ends_a], tail_w)
    gate_a[: sources * FULL] = ends_a[0].astype(F32)
    full_b = [[block(ref, base + b * SUB, SUB) for b in range(half)] for ref in refs]
    low_b = mm(full_b[0] + full_b[1], weight(0, half * LANES))
    high_b = mm(
        full_b[0][:-1] + full_b[1][:-1], weight(half * LANES, whole - half * LANES)
    ) + mm([x[-1][:, :tail] for x in full_b], tail_w)
    gate_b[: sources * SUB] = full_b[0][-1].astype(F32)
    for n in range(columns):
        at = slice(n * LANES, (n + 1) * LANES)
        part_a[n, : sources * FULL] = out_a[:, at]
        part_b[0, n, : sources * SUB] = low_b[:, at]
        part_b[1, n, : sources * SUB] = high_b[:, at]

    lane = lax.broadcasted_iota(jnp.int32, (sources, LANES), 1)
    dots = jnp.zeros((sources, LANES), F32)
    for s in range(act_ref.shape[0]):
        total = jnp.zeros((sources, LANES), F32)
        if s < FULL:
            gate = gate_a[pl.ds(s, sources, stride=FULL), :]
        else:
            gate = gate_b[pl.ds(s - FULL + SUB // 2, sources, stride=SUB), :]
        gate = jnp.broadcast_to(gate[:, tail : tail + 1], (sources, LANES))
        for n in range(columns):
            if s < FULL:
                proj = part_a[n, pl.ds(s, sources, stride=FULL), :]
            else:
                proj = (
                    part_b[0, n, pl.ds(s - FULL, sources, stride=SUB), :]
                    + part_b[1, n, pl.ds(s - FULL + SUB // 2, sources, stride=SUB), :]
                )
            at = slice(n * LANES, (n + 1) * LANES)
            grad_ref[s, :, at] = (gate * proj).astype(BF16)
            total = total + act_ref[s, :, at].astype(F32) * proj
        dots = jnp.where(lane == s, jnp.sum(total, axis=1, keepdims=True), dots)
    dots_ref[...] = dots


def collect_kernel(slots, ids_ref, rank_ref, mine_ref, out_ref):
    experts, tokens = rank_ref.shape
    rank = rank_ref[...]
    back = mine_ref[...]
    found = jnp.zeros((experts, tokens), F32)
    for s in range(slots):
        found = jnp.where(rank == float(s), back[:, s : s + 1], found)
    ids = ids_ref[...]
    expert = lax.broadcasted_iota(jnp.int32, (experts, tokens), 0)
    for k in range(ids.shape[0]):
        out_ref[k : k + 1, :] = jnp.sum(
            jnp.where(ids[k : k + 1, :] == expert, found, 0.0), axis=0, keepdims=True
        )


VMEM = pl.BlockSpec(memory_space=pltpu.VMEM)
PARAMS = pltpu.CompilerParams(vmem_limit_bytes=16 * 1024 * 1024)


def on_device(cotangent, route_weight, expert_ids, down_weight, hidden_act):
    experts = lax.axis_size("expert")
    tokens, width = cotangent.shape
    topk = expert_ids.shape[1]
    _, _, _, slots, hidden = hidden_act.shape
    blocks = -(-width // LANES)
    rows = blocks * FULL + blocks // 2 * SUB
    ids = expert_ids.T
    send, rank = pl.pallas_call(
        pack_kernel,
        out_shape=(
            jax.ShapeDtypeStruct((experts, rows, LANES), BF16),
            jax.ShapeDtypeStruct((experts, tokens), F32),
        ),
        in_specs=[VMEM] * 3,
        out_specs=(VMEM, VMEM),
        compiler_params=PARAMS,
        name="pack",
    )(ids, route_weight.T, cotangent.T)
    own = lax.all_to_all(send, "expert", split_axis=0, concat_axis=0, tiled=True)
    other = lax.ppermute(own, "fsdp", [(0, 1), (1, 0)])
    core = lax.axis_index("fsdp").astype(jnp.int32).reshape(1)
    grad, dots = pl.pallas_call(
        project_kernel,
        out_shape=(
            jax.ShapeDtypeStruct((slots, experts, hidden), BF16),
            jax.ShapeDtypeStruct((experts, LANES), F32),
        ),
        in_specs=[pl.BlockSpec(memory_space=pltpu.SMEM)] + [VMEM] * 4,
        out_specs=(VMEM, VMEM),
        scratch_shapes=[
            pltpu.VMEM((hidden // LANES, (experts + 1) * FULL, LANES), F32),
            pltpu.VMEM((2, hidden // LANES, (experts + 1) * SUB, LANES), F32),
            pltpu.VMEM(((experts + 1) * FULL, LANES), F32),
            pltpu.VMEM(((experts + 1) * SUB, LANES), F32),
        ],
        compiler_params=PARAMS,
        name="project",
    )(core, own, other, down_weight[0].T, hidden_act[0, 0].swapaxes(0, 1))
    whole = dots + lax.ppermute(dots, "fsdp", [(0, 1), (1, 0)])
    back = lax.all_to_all(
        whole.reshape(experts, 1, LANES), "expert", split_axis=0, concat_axis=0, tiled=True
    ).reshape(experts, LANES)
    route_grad = pl.pallas_call(
        lambda *refs: collect_kernel(slots, *refs),
        out_shape=jax.ShapeDtypeStruct((topk, tokens), F32),
        in_specs=[VMEM] * 3,
        out_specs=VMEM,
        compiler_params=PARAMS,
        name="collect",
    )(ids, rank, back)
    return grad.swapaxes(0, 1)[None, None], route_grad.T


def solution(mesh):
    placed = (
        P(("dp", "expert"), "fsdp"),
        P(("dp", "expert"), None),
        P(("dp", "expert"), None),
        P("expert", "fsdp", None),
        P("dp", "expert", None, None, "fsdp"),
    )
    return jax.shard_map(
        on_device,
        mesh=mesh,
        in_specs=placed,
        out_specs=(P("dp", "expert", None, None, "fsdp"), P(("dp", "expert"), None)),
        check_vma=False,
    )
```

```python
import jax
import jax.numpy as jnp
from jax import lax
from jax.experimental import pallas as pl
from jax.experimental.pallas import tpu as pltpu
from jax.sharding import PartitionSpec as P

LANES = 128
SUB = 8
FULL = 16
F32 = jnp.float32
BF16 = jnp.bfloat16
NT = (((1,), (1,)), ((), ()))
NN = (((1,), (0,)), ((), ()))


def ranks(ids, experts):
    topk, tokens = ids.shape
    expert = lax.broadcasted_iota(jnp.int32, (experts, tokens), 0)
    hit = jnp.zeros((experts, tokens), F32)
    for k in range(topk):
        hit = hit + (ids[k : k + 1, :] == expert).astype(F32)
    earlier = lax.broadcasted_iota(jnp.int32, (tokens, tokens), 0) < lax.broadcasted_iota(
        jnp.int32, (tokens, tokens), 1
    )
    before = lax.dot_general(
        hit.astype(BF16), earlier.astype(F32).astype(BF16), NN, preferred_element_type=F32
    )
    return jnp.where(hit > 0.5, before, -1.0)


def pack_kernel(
    ids_hbm, weight_hbm, cot_hbm, sent_hbm, rank_ref, ids_ref, weight_ref, cot_ref, send_ref, in_sems, out_sems
):
    inputs = [
        pltpu.make_async_copy(src, dst, in_sems.at[i])
        for i, (src, dst) in enumerate(
            ((ids_hbm, ids_ref), (weight_hbm, weight_ref), (cot_hbm, cot_ref))
        )
    ]
    for copy in inputs:
        copy.start()
    outputs = []
    experts = send_ref.shape[0]
    width, tokens = cot_ref.shape
    blocks = -(-width // LANES)
    half = blocks // 2
    whole = width // LANES * LANES
    inputs[0].wait()
    inputs[1].wait()
    ids = ids_ref[...]
    rank = ranks(ids, experts)
    rank_ref[...] = rank
    expert = lax.broadcasted_iota(jnp.int32, (experts, tokens), 0)
    gate = jnp.zeros((experts, tokens), F32)
    for k in range(ids.shape[0]):
        gate = gate + jnp.where(
            ids[k : k + 1, :] == expert, weight_ref[k : k + 1, :].astype(F32), 0.0
        )

    inputs[2].wait()
    cot = cot_ref[...]
    tail = jnp.concatenate(
        [cot[whole:], jnp.zeros((LANES - (width - whole), tokens), BF16)], axis=0
    )
    free = (
        lax.broadcasted_iota(jnp.int32, (LANES, tokens), 0) >= width - whole
    ).astype(F32).astype(BF16)

    def pick(rows, columns):
        return lax.dot_general(rows, columns, NT, preferred_element_type=F32)

    def put(first, count, value):
        send_ref[:, first : first + count, :] = value.astype(BF16).reshape(experts, count, LANES)

    def ship(first, count):
        at = (slice(None), slice(first, first + count), slice(None))
        copy = pltpu.make_async_copy(send_ref.at[at], sent_hbm.at[at], out_sems.at[len(outputs)])
        copy.start()
        outputs.append(copy)

    def select(count, wanted):
        rows = lax.broadcasted_iota(jnp.int32, (experts, count, tokens), 1)
        chosen = (rank[:, None, :] == wanted(rows).astype(F32)).astype(F32)
        gated = chosen * gate[:, None, :]
        return (
            chosen.reshape(experts * count, tokens).astype(BF16),
            gated.reshape(experts * count, tokens).astype(BF16),
        )

    rows_a, gated_a = select(FULL, lambda r: r)
    for b in range(blocks - 1):
        put(b * FULL, FULL, pick(rows_a, cot[b * LANES : (b + 1) * LANES]))
        ship(b * FULL, FULL)
    put((blocks - 1) * FULL, FULL, pick(rows_a, tail) + pick(gated_a, free))
    ship((blocks - 1) * FULL, FULL)

    base = blocks * FULL
    rows_l, _ = select(SUB, lambda r: jnp.where(r < SUB // 2, r + FULL, -2))
    rows_h, gated_h = select(SUB, lambda r: jnp.where(r < SUB // 2, -2, r + FULL - SUB // 2))
    for b in range(half):
        low = pick(rows_l, cot[b * LANES : (b + 1) * LANES])
        if half + b < blocks - 1:
            high = pick(rows_h, cot[(half + b) * LANES : (half + b + 1) * LANES])
        else:
            high = pick(rows_h, tail) + pick(gated_h, free)
        put(base + b * SUB, SUB, low + high)
        if b % 2:
            ship(base + (b - 1) * SUB, 2 * SUB)
    for copy in outputs:
        copy.wait()


def align_kernel(core_ref, act_ref, act_other_ref, weight_ref, weight_other_ref, out_ref):
    slots, sources, hidden = act_ref.shape
    width = weight_ref.shape[0] // 2
    blocks = -(-width // LANES)
    half = blocks // 2
    rows = out_ref.shape[0] // sources
    start = core_ref[0] * width
    acts = [ref[...].reshape(slots * sources, hidden) for ref in (act_ref, act_other_ref)]
    for first in range(0, blocks, 2):
        at, count = first * LANES, min(2 * LANES, width - first * LANES)
        out = jnp.zeros((slots * sources, 2 * LANES), F32)
        for act, ref in zip(acts, (weight_ref, weight_other_ref)):
            columns = ref[pl.ds(pl.multiple_of(start + at, 16), count), :]
            if count < 2 * LANES:
                columns = jnp.concatenate(
                    [columns, jnp.zeros((2 * LANES - count, hidden), BF16)], axis=0
                )
            out = out + lax.dot_general(act, columns, NT, preferred_element_type=F32)
        for b in (first, first + 1):
            for s in range(slots):
                if s < FULL:
                    row = b * FULL + s
                else:
                    row = blocks * FULL + b % half * SUB + b // half * (SUB // 2) + s - FULL
                out_ref[pl.ds(row, sources, stride=rows), :] = out[
                    s * sources : (s + 1) * sources, (b - first) * LANES : (b - first + 1) * LANES
                ]


def dots_kernel(blocks, rows_ref, aligned_hbm, dots_ref, aligned_ref, sems):
    sources = rows_ref.shape[0]
    parts = sems.shape[0]
    step = sources // parts
    copies = [
        pltpu.make_async_copy(
            aligned_hbm.at[pl.ds(p * step, step)], aligned_ref.at[pl.ds(p * step, step)], sems.at[p]
        )
        for p in range(parts)
    ]
    for copy in copies:
        copy.start()

    def reduce(p, first, count, steps):
        total = jnp.zeros((step, count, LANES), F32)
        of = slice(p * step, (p + 1) * step)
        for b in range(steps):
            at = slice(first + b * count, first + (b + 1) * count)
            total = total + rows_ref[of, at, :].astype(F32) * aligned_ref[of, at, :]
        return jnp.sum(total, axis=2, keepdims=True)

    def spread(value, count, slot):
        lane = lax.broadcasted_iota(jnp.int32, (step, count, LANES), 2)
        row = lax.broadcasted_iota(jnp.int32, (step, count, LANES), 1)
        return jnp.sum(jnp.where(lane == slot(row), value, 0.0), axis=1)

    for p in range(parts):
        copies[p].wait()
        full = spread(reduce(p, 0, FULL, blocks), FULL, lambda r: r)
        split = spread(
            reduce(p, blocks * FULL, SUB, blocks // 2),
            SUB,
            lambda r: jnp.where(r < SUB // 2, r, r - SUB // 2) + FULL,
        )
        dots_ref[p * step : (p + 1) * step, :] = full + split


def project_kernel(
    core_ref, own_ref, other_ref, weight_ref, grad_ref, part_a, part_b, gate_a, gate_b
):
    sources = own_ref.shape[0]
    depth, hidden = weight_ref.shape
    width = depth // 2
    blocks = -(-width // LANES)
    half = blocks // 2
    whole = width // LANES * LANES
    tail = width - whole
    base = blocks * FULL
    columns = hidden // LANES
    core = core_ref[0]
    mine = core * width
    theirs = width - mine

    def block(ref, first, count):
        return ref[:, first : first + count, :].reshape(sources * count, LANES)

    def weight(first, count):
        return [
            weight_ref[pl.ds(pl.multiple_of(start + first, 16), count), :] for start in (mine, theirs)
        ]

    def mm(rows, columns_):
        return lax.dot_general(
            jnp.concatenate(rows, axis=1),
            jnp.concatenate(columns_, axis=0),
            NN,
            preferred_element_type=F32,
        )

    refs = (own_ref, other_ref)
    tail_w = weight(whole, tail)
    full_a = [[block(ref, b * FULL, FULL) for b in range(blocks - 1)] for ref in refs]
    ends_a = [block(ref, (blocks - 1) * FULL, FULL) for ref in refs]
    out_a = mm(full_a[0] + full_a[1], weight(0, whole)) + mm([x[:, :tail] for x in ends_a], tail_w)
    gate_a[: sources * FULL] = ends_a[0].astype(F32)
    full_b = [[block(ref, base + b * SUB, SUB) for b in range(half)] for ref in refs]
    low_b = mm(full_b[0] + full_b[1], weight(0, half * LANES))
    high_b = mm(
        full_b[0][:-1] + full_b[1][:-1], weight(half * LANES, whole - half * LANES)
    ) + mm([x[-1][:, :tail] for x in full_b], tail_w)
    gate_b[: sources * SUB] = full_b[0][-1].astype(F32)
    for n in range(columns):
        at = slice(n * LANES, (n + 1) * LANES)
        part_a[n, : sources * FULL] = out_a[:, at]
        part_b[0, n, : sources * SUB] = low_b[:, at]
        part_b[1, n, : sources * SUB] = high_b[:, at]

    for s in range(grad_ref.shape[0]):
        if s < FULL:
            gate = gate_a[pl.ds(s, sources, stride=FULL), :]
        else:
            gate = gate_b[pl.ds(s - FULL + SUB // 2, sources, stride=SUB), :]
        gate = jnp.broadcast_to(gate[:, tail : tail + 1], (sources, LANES))
        for n in range(columns):
            if s < FULL:
                proj = part_a[n, pl.ds(s, sources, stride=FULL), :]
            else:
                proj = (
                    part_b[0, n, pl.ds(s - FULL, sources, stride=SUB), :]
                    + part_b[1, n, pl.ds(s - FULL + SUB // 2, sources, stride=SUB), :]
                )
            at = slice(n * LANES, (n + 1) * LANES)
            grad_ref[s, :, at] = (gate * proj).astype(BF16)


def collect_kernel(slots, ids_ref, rank_ref, mine_ref, out_ref):
    experts, tokens = rank_ref.shape
    rank = rank_ref[...]
    back = mine_ref[...]
    found = jnp.zeros((experts, tokens), F32)
    for s in range(slots):
        found = jnp.where(rank == float(s), back[:, s : s + 1], found)
    ids = ids_ref[...]
    expert = lax.broadcasted_iota(jnp.int32, (experts, tokens), 0)
    for k in range(ids.shape[0]):
        out_ref[k : k + 1, :] = jnp.sum(
            jnp.where(ids[k : k + 1, :] == expert, found, 0.0), axis=0, keepdims=True
        )


VMEM = pl.BlockSpec(memory_space=pltpu.VMEM)
HBM = pl.BlockSpec(memory_space=pltpu.HBM)
WHOLE = pltpu.CompilerParams(vmem_limit_bytes=64 * 1024 * 1024 - 128 * 1024)
MOST = pltpu.CompilerParams(vmem_limit_bytes=54 * 1000 * 1000)
PARAMS = pltpu.CompilerParams(vmem_limit_bytes=16 * 1024 * 1024)


def on_device(cotangent, route_weight, expert_ids, down_weight, hidden_act):
    experts = lax.axis_size("expert")
    tokens, width = cotangent.shape
    topk = expert_ids.shape[1]
    _, _, _, slots, hidden = hidden_act.shape
    blocks = -(-width // LANES)
    rows = blocks * FULL + blocks // 2 * SUB
    ids = expert_ids.T
    send, rank = pl.pallas_call(
        pack_kernel,
        out_shape=(
            jax.ShapeDtypeStruct((experts, rows, LANES), BF16),
            jax.ShapeDtypeStruct((experts, tokens), F32),
        ),
        in_specs=[HBM] * 3,
        out_specs=(HBM, VMEM),
        scratch_shapes=[
            pltpu.VMEM((topk, tokens), jnp.int32),
            pltpu.VMEM((topk, tokens), BF16),
            pltpu.VMEM((width, tokens), BF16),
            pltpu.VMEM((experts, rows, LANES), BF16),
            pltpu.SemaphoreType.DMA((3,)),
            pltpu.SemaphoreType.DMA((blocks + blocks // 4,)),
        ],
        compiler_params=WHOLE,
        name="pack",
    )(ids, route_weight.T, cotangent.T)
    weight, send = lax.optimization_barrier((down_weight[0].T, send))
    own = lax.all_to_all(send, "expert", split_axis=0, concat_axis=0, tiled=True)
    swap = [(0, 1), (1, 0)]
    core = lax.axis_index("fsdp").astype(jnp.int32).reshape(1)
    act = hidden_act[0, 0].swapaxes(0, 1)
    scalar = pl.BlockSpec(memory_space=pltpu.SMEM)
    act_other = lax.ppermute(act, "fsdp", swap)
    weight_other = lax.ppermute(weight, "fsdp", swap)
    both = pl.pallas_call(
        align_kernel,
        out_shape=jax.ShapeDtypeStruct((experts * rows, LANES), F32),
        in_specs=[scalar] + [VMEM] * 4,
        out_specs=VMEM,
        compiler_params=PARAMS,
        cost_estimate=pl.CostEstimate(
            flops=2 * slots * experts * weight.size, bytes_accessed=16 * 1024 * 1024, transcendentals=0
        ),
        name="align",
    )(core, act, act_other, weight, weight_other).reshape(experts, rows, LANES)
    dots = pl.pallas_call(
        lambda *refs: dots_kernel(blocks, *refs),
        out_shape=jax.ShapeDtypeStruct((experts, LANES), F32),
        in_specs=[VMEM, HBM],
        out_specs=VMEM,
        scratch_shapes=[
            pltpu.VMEM((experts, rows, LANES), F32),
            pltpu.SemaphoreType.DMA((experts // SUB,)),
        ],
        compiler_params=MOST,
        name="dots",
    )(own, both)
    own, dots = lax.optimization_barrier((own, dots))
    whole = dots + lax.ppermute(dots, "fsdp", swap)
    back = lax.all_to_all(
        whole.reshape(experts, 1, LANES), "expert", split_axis=0, concat_axis=0, tiled=True
    ).reshape(experts, LANES)
    other = lax.ppermute(own, "fsdp", swap)
    grad = pl.pallas_call(
        project_kernel,
        out_shape=jax.ShapeDtypeStruct((slots, experts, hidden), BF16),
        in_specs=[scalar] + [VMEM] * 3,
        out_specs=VMEM,
        scratch_shapes=[
            pltpu.VMEM((hidden // LANES, (experts + 1) * FULL, LANES), F32),
            pltpu.VMEM((2, hidden // LANES, (experts + 1) * SUB, LANES), F32),
            pltpu.VMEM(((experts + 1) * FULL, LANES), F32),
            pltpu.VMEM(((experts + 1) * SUB, LANES), F32),
        ],
        compiler_params=PARAMS,
        cost_estimate=pl.CostEstimate(
            flops=2 * slots * experts * weight.size, bytes_accessed=10 * 1024 * 1024, transcendentals=0
        ),
        name="project",
    )(core, own, other, weight)
    back, grad = lax.optimization_barrier((back, grad))
    route_grad = pl.pallas_call(
        lambda *refs: collect_kernel(slots, *refs),
        out_shape=jax.ShapeDtypeStruct((topk, tokens), F32),
        in_specs=[VMEM] * 3,
        out_specs=VMEM,
        compiler_params=PARAMS,
        name="collect",
    )(ids, rank, back)
    return grad.swapaxes(0, 1)[None, None], route_grad.T


def solution(mesh):
    placed = (
        P(("dp", "expert"), "fsdp"),
        P(("dp", "expert"), None),
        P(("dp", "expert"), None),
        P("expert", "fsdp", None),
        P("dp", "expert", None, None, "fsdp"),
    )
    return jax.shard_map(
        on_device,
        mesh=mesh,
        in_specs=placed,
        out_specs=(P("dp", "expert", None, None, "fsdp"), P(("dp", "expert"), None)),
        check_vma=False,
    )
```

```python
import jax
import jax.numpy as jnp
from jax import lax
from jax.experimental import pallas as pl
from jax.experimental.pallas import tpu as pltpu
from jax.sharding import PartitionSpec as P

LANES = 128
SUB = 8
FULL = 16
F32 = jnp.float32
BF16 = jnp.bfloat16
NT = (((1,), (1,)), ((), ()))
NN = (((1,), (0,)), ((), ()))


def ranks(ids, experts):
    topk, tokens = ids.shape
    expert = lax.broadcasted_iota(jnp.int32, (experts, tokens), 0)
    hit = jnp.zeros((experts, tokens), F32)
    for k in range(topk):
        hit = hit + (ids[k : k + 1, :] == expert).astype(F32)
    earlier = lax.broadcasted_iota(jnp.int32, (tokens, tokens), 0) < lax.broadcasted_iota(
        jnp.int32, (tokens, tokens), 1
    )
    before = lax.dot_general(
        hit.astype(BF16), earlier.astype(F32).astype(BF16), NN, preferred_element_type=F32
    )
    return jnp.where(hit > 0.5, before, -1.0)


def pack_kernel(
    ids_hbm, weight_hbm, cot_hbm, sent_hbm, rank_ref, ids_ref, weight_ref, cot_ref, send_ref, in_sems, out_sems
):
    inputs = [
        pltpu.make_async_copy(src, dst, in_sems.at[i])
        for i, (src, dst) in enumerate(
            ((ids_hbm, ids_ref), (weight_hbm, weight_ref), (cot_hbm, cot_ref))
        )
    ]
    for copy in inputs:
        copy.start()
    outputs = []
    experts = send_ref.shape[0]
    width, tokens = cot_ref.shape
    blocks = -(-width // LANES)
    half = blocks // 2
    whole = width // LANES * LANES
    inputs[0].wait()
    inputs[1].wait()
    ids = ids_ref[...]
    rank = ranks(ids, experts)
    rank_ref[...] = rank
    expert = lax.broadcasted_iota(jnp.int32, (experts, tokens), 0)
    gate = jnp.zeros((experts, tokens), F32)
    for k in range(ids.shape[0]):
        gate = gate + jnp.where(
            ids[k : k + 1, :] == expert, weight_ref[k : k + 1, :].astype(F32), 0.0
        )

    inputs[2].wait()
    cot = cot_ref[...]
    tail = jnp.concatenate(
        [cot[whole:], jnp.zeros((LANES - (width - whole), tokens), BF16)], axis=0
    )
    free = (
        lax.broadcasted_iota(jnp.int32, (LANES, tokens), 0) >= width - whole
    ).astype(F32).astype(BF16)

    def pick(rows, columns):
        return lax.dot_general(rows, columns, NT, preferred_element_type=F32)

    def put(first, count, value):
        send_ref[:, first : first + count, :] = value.astype(BF16).reshape(experts, count, LANES)

    def ship(first, count):
        at = (slice(None), slice(first, first + count), slice(None))
        copy = pltpu.make_async_copy(send_ref.at[at], sent_hbm.at[at], out_sems.at[len(outputs)])
        copy.start()
        outputs.append(copy)

    def select(count, wanted):
        rows = lax.broadcasted_iota(jnp.int32, (experts, count, tokens), 1)
        chosen = (rank[:, None, :] == wanted(rows).astype(F32)).astype(F32)
        gated = chosen * gate[:, None, :]
        return (
            chosen.reshape(experts * count, tokens).astype(BF16),
            gated.reshape(experts * count, tokens).astype(BF16),
        )

    rows_a, gated_a = select(FULL, lambda r: r)
    for b in range(blocks - 1):
        put(b * FULL, FULL, pick(rows_a, cot[b * LANES : (b + 1) * LANES]))
        ship(b * FULL, FULL)
    put((blocks - 1) * FULL, FULL, pick(rows_a, tail) + pick(gated_a, free))
    ship((blocks - 1) * FULL, FULL)

    base = blocks * FULL
    rows_l, _ = select(SUB, lambda r: jnp.where(r < SUB // 2, r + FULL, -2))
    rows_h, gated_h = select(SUB, lambda r: jnp.where(r < SUB // 2, -2, r + FULL - SUB // 2))
    for b in range(half):
        low = pick(rows_l, cot[b * LANES : (b + 1) * LANES])
        if half + b < blocks - 1:
            high = pick(rows_h, cot[(half + b) * LANES : (half + b + 1) * LANES])
        else:
            high = pick(rows_h, tail) + pick(gated_h, free)
        put(base + b * SUB, SUB, low + high)
        if b % 2:
            ship(base + (b - 1) * SUB, 2 * SUB)
    for copy in outputs:
        copy.wait()


def align_kernel(core_ref, act_ref, act_other_ref, weight_ref, weight_other_ref, out_ref):
    slots, sources, hidden = act_ref.shape
    width = weight_ref.shape[0] // 2
    blocks = -(-width // LANES)
    half = blocks // 2
    rows = out_ref.shape[0] // sources
    start = core_ref[0] * width
    acts = [ref[...].reshape(slots * sources, hidden) for ref in (act_ref, act_other_ref)]
    for first in range(0, blocks, 2):
        at, count = first * LANES, min(2 * LANES, width - first * LANES)
        out = jnp.zeros((slots * sources, 2 * LANES), F32)
        for act, ref in zip(acts, (weight_ref, weight_other_ref)):
            columns = ref[pl.ds(pl.multiple_of(start + at, 16), count), :]
            if count < 2 * LANES:
                columns = jnp.concatenate(
                    [columns, jnp.zeros((2 * LANES - count, hidden), BF16)], axis=0
                )
            out = out + lax.dot_general(act, columns, NT, preferred_element_type=F32)
        for b in (first, first + 1):
            for s in range(slots):
                if s < FULL:
                    row = b * FULL + s
                else:
                    row = blocks * FULL + b % half * SUB + b // half * (SUB // 2) + s - FULL
                out_ref[pl.ds(row, sources, stride=rows), :] = out[
                    s * sources : (s + 1) * sources, (b - first) * LANES : (b - first + 1) * LANES
                ]


def dots_kernel(blocks, rows_ref, aligned_hbm, dots_ref, aligned_ref, sems):
    sources = rows_ref.shape[0]
    parts = sems.shape[0]
    step = sources // parts
    copies = [
        pltpu.make_async_copy(
            aligned_hbm.at[pl.ds(p * step, step)], aligned_ref.at[pl.ds(p * step, step)], sems.at[p]
        )
        for p in range(parts)
    ]
    for copy in copies:
        copy.start()

    def reduce(p, first, count, steps):
        total = jnp.zeros((step, count, LANES), F32)
        of = slice(p * step, (p + 1) * step)
        for b in range(steps):
            at = slice(first + b * count, first + (b + 1) * count)
            total = total + rows_ref[of, at, :].astype(F32) * aligned_ref[of, at, :]
        return jnp.sum(total, axis=2, keepdims=True)

    def spread(value, count, slot):
        lane = lax.broadcasted_iota(jnp.int32, (step, count, LANES), 2)
        row = lax.broadcasted_iota(jnp.int32, (step, count, LANES), 1)
        return jnp.sum(jnp.where(lane == slot(row), value, 0.0), axis=1)

    for p in range(parts):
        copies[p].wait()
        full = spread(reduce(p, 0, FULL, blocks), FULL, lambda r: r)
        split = spread(
            reduce(p, blocks * FULL, SUB, blocks // 2),
            SUB,
            lambda r: jnp.where(r < SUB // 2, r, r - SUB // 2) + FULL,
        )
        for first in (p * step, sources + p * step):
            dots_ref[first : first + step, 0, :] = full + split


def project_kernel(
    core_ref, own_ref, other_ref, weight_hbm, grad_hbm, weight_ref, grad_ref, part, tails, gates, in_sems, out_sems
):
    sources = own_ref.shape[0]
    parts, depth, columns = weight_ref.shape
    width = depth // 2
    blocks = -(-width // LANES)
    half = blocks // 2
    whole = width // LANES * LANES
    tail = width - whole
    base = blocks * FULL
    split = sources * FULL
    core = core_ref[0]
    mine = core * width
    theirs = width - mine

    def columns_of(p):
        return slice(p * columns, (p + 1) * columns)

    inputs = [
        pltpu.make_async_copy(weight_hbm.at[:, columns_of(p)], weight_ref.at[p], in_sems.at[p])
        for p in range(parts)
    ]
    for copy in inputs:
        copy.start()

    def block(ref, b):
        full = ref[:, b * FULL : (b + 1) * FULL, :].reshape(split, LANES)
        at = base + b % half * SUB
        return jnp.concatenate([full, ref[:, at : at + SUB, :].reshape(sources * SUB, LANES)], axis=0)

    refs = (own_ref, other_ref)
    ends = [block(ref, blocks - 1) for ref in refs]
    low = jnp.concatenate([block(ref, b) for ref in refs for b in range(half)], axis=1)
    high = jnp.concatenate([block(ref, b) for ref in refs for b in range(half, blocks - 1)], axis=1)
    last = jnp.concatenate([x[:, :tail] for x in ends], axis=1)
    gates[: ends[0].shape[0]] = ends[0].astype(F32)
    outputs = []
    for p in range(parts):
        inputs[p].wait()

        def mm(rows, first, count):
            return lax.dot_general(
                rows,
                jnp.concatenate(
                    [
                        weight_ref[p, pl.ds(pl.multiple_of(start + first, 16), count), :]
                        for start in (mine, theirs)
                    ],
                    axis=0,
                ),
                NN,
                preferred_element_type=F32,
            )

        lows = mm(low, 0, half * LANES)
        highs = mm(high, half * LANES, whole - half * LANES) + mm(last, whole, tail)
        for n in range(columns // LANES):
            at = slice(n * LANES, (n + 1) * LANES)
            part[n, :split] = lows[:split, at] + highs[:split, at]
            tails[0, n, : sources * SUB] = lows[split:, at]
            tails[1, n, : sources * SUB] = highs[split:, at]
        for s in range(grad_ref.shape[0]):
            if s < FULL:
                gate = gates[pl.ds(s, sources, stride=FULL), :]
            else:
                gate = gates[pl.ds(split + s - FULL + SUB // 2, sources, stride=SUB), :]
            gate = jnp.broadcast_to(gate[:, tail : tail + 1], (sources, LANES))
            for n in range(columns // LANES):
                if s < FULL:
                    proj = part[n, pl.ds(s, sources, stride=FULL), :]
                else:
                    proj = (
                        tails[0, n, pl.ds(s - FULL, sources, stride=SUB), :]
                        + tails[1, n, pl.ds(s - FULL + SUB // 2, sources, stride=SUB), :]
                    )
                at = slice(p * columns + n * LANES, p * columns + (n + 1) * LANES)
                grad_ref[s, :, at] = (gate * proj).astype(BF16)
        copy = pltpu.make_async_copy(
            grad_ref.at[:, :, columns_of(p)], grad_hbm.at[:, :, columns_of(p)], out_sems.at[p]
        )
        copy.start()
        outputs.append(copy)
    for copy in outputs:
        copy.wait()


def collect_kernel(slots, ids_ref, rank_ref, mine_ref, out_ref):
    experts, tokens = rank_ref.shape
    rank = rank_ref[...]
    back = mine_ref[:experts, :] + mine_ref[experts:, :]
    found = jnp.zeros((experts, tokens), F32)
    for s in range(slots):
        found = jnp.where(rank == float(s), back[:, s : s + 1], found)
    ids = ids_ref[...]
    expert = lax.broadcasted_iota(jnp.int32, (experts, tokens), 0)
    for k in range(ids.shape[0]):
        out_ref[k : k + 1, :] = jnp.sum(
            jnp.where(ids[k : k + 1, :] == expert, found, 0.0), axis=0, keepdims=True
        )


VMEM = pl.BlockSpec(memory_space=pltpu.VMEM)
HBM = pl.BlockSpec(memory_space=pltpu.HBM)
WHOLE = pltpu.CompilerParams(vmem_limit_bytes=64 * 1024 * 1024 - 128 * 1024)
MOST = pltpu.CompilerParams(vmem_limit_bytes=54 * 1000 * 1000)

PARAMS = pltpu.CompilerParams(vmem_limit_bytes=16 * 1024 * 1024)


def on_device(cotangent, route_weight, expert_ids, down_weight, hidden_act):
    experts = lax.axis_size("expert")
    tokens, width = cotangent.shape
    topk = expert_ids.shape[1]
    _, _, _, slots, hidden = hidden_act.shape
    blocks = -(-width // LANES)
    rows = blocks * FULL + blocks // 2 * SUB
    ids = expert_ids.T
    send, rank = pl.pallas_call(
        pack_kernel,
        out_shape=(
            jax.ShapeDtypeStruct((experts, rows, LANES), BF16),
            jax.ShapeDtypeStruct((experts, tokens), F32),
        ),
        in_specs=[HBM] * 3,
        out_specs=(HBM, VMEM),
        scratch_shapes=[
            pltpu.VMEM((topk, tokens), jnp.int32),
            pltpu.VMEM((topk, tokens), BF16),
            pltpu.VMEM((width, tokens), BF16),
            pltpu.VMEM((experts, rows, LANES), BF16),
            pltpu.SemaphoreType.DMA((3,)),
            pltpu.SemaphoreType.DMA((blocks + blocks // 4,)),
        ],
        compiler_params=WHOLE,
        name="pack",
    )(ids, route_weight.T, cotangent.T)
    weight, send = lax.optimization_barrier((down_weight[0].T, send))
    own = lax.all_to_all(send, "expert", split_axis=0, concat_axis=0, tiled=True)
    swap = [(0, 1), (1, 0)]
    core = lax.axis_index("fsdp").astype(jnp.int32).reshape(1)
    act = hidden_act[0, 0].swapaxes(0, 1)
    scalar = pl.BlockSpec(memory_space=pltpu.SMEM)
    act_other = lax.ppermute(act, "fsdp", swap)
    weight_other = lax.ppermute(weight, "fsdp", swap)
    both = pl.pallas_call(
        align_kernel,
        out_shape=jax.ShapeDtypeStruct((experts * rows, LANES), F32),
        in_specs=[scalar] + [VMEM] * 4,
        out_specs=VMEM,
        compiler_params=PARAMS,
        cost_estimate=pl.CostEstimate(
            flops=2 * slots * experts * weight.size, bytes_accessed=16 * 1024 * 1024, transcendentals=0
        ),
        name="align",
    )(core, act, act_other, weight, weight_other).reshape(experts, rows, LANES)
    dots = pl.pallas_call(
        lambda *refs: dots_kernel(blocks, *refs),
        out_shape=jax.ShapeDtypeStruct((2 * experts, 1, LANES), F32),
        in_specs=[VMEM, HBM],
        out_specs=VMEM,
        scratch_shapes=[
            pltpu.VMEM((experts, rows, LANES), F32),
            pltpu.SemaphoreType.DMA((experts // SUB,)),
        ],
        compiler_params=MOST,
        name="dots",
    )(own, both)
    own, dots = lax.optimization_barrier((own, dots))
    back = lax.all_to_all(dots, ("fsdp", "expert"), split_axis=0, concat_axis=0, tiled=True)
    back = back.reshape(2 * experts, LANES)
    other = lax.ppermute(own, "fsdp", swap)
    parts = hidden // (2 * LANES)
    grad = pl.pallas_call(
        project_kernel,
        out_shape=jax.ShapeDtypeStruct((slots, experts, hidden), BF16),
        in_specs=[scalar, VMEM, VMEM, HBM],
        out_specs=HBM,
        scratch_shapes=[
            pltpu.VMEM((parts, weight.shape[0], hidden // parts), BF16),
            pltpu.VMEM((slots, experts, hidden), BF16),
            pltpu.VMEM((hidden // parts // LANES, (experts + 1) * FULL, LANES), F32),
            pltpu.VMEM((2, hidden // parts // LANES, (experts + 1) * SUB, LANES), F32),
            pltpu.VMEM(((experts + 1) * FULL + experts * SUB, LANES), F32),
            pltpu.SemaphoreType.DMA((parts,)),
            pltpu.SemaphoreType.DMA((parts,)),
        ],
        compiler_params=MOST,
        cost_estimate=pl.CostEstimate(
            flops=2 * slots * experts * weight.size, bytes_accessed=10 * 1024 * 1024, transcendentals=0
        ),
        name="project",
    )(core, own, other, weight)
    back, grad = lax.optimization_barrier((back, grad))
    route_grad = pl.pallas_call(
        lambda *refs: collect_kernel(slots, *refs),
        out_shape=jax.ShapeDtypeStruct((topk, tokens), F32),
        in_specs=[VMEM] * 3,
        out_specs=VMEM,
        compiler_params=PARAMS,
        name="collect",
    )(ids, rank, back)
    return grad.swapaxes(0, 1)[None, None], route_grad.T


def solution(mesh):
    placed = (
        P(("dp", "expert"), "fsdp"),
        P(("dp", "expert"), None),
        P(("dp", "expert"), None),
        P("expert", "fsdp", None),
        P("dp", "expert", None, None, "fsdp"),
    )
    return jax.shard_map(
        on_device,
        mesh=mesh,
        in_specs=placed,
        out_specs=(P("dp", "expert", None, None, "fsdp"), P(("dp", "expert"), None)),
        check_vma=False,
    )
```

```python
import jax
import jax.numpy as jnp
from jax import lax
from jax.experimental import pallas as pl
from jax.experimental.pallas import tpu as pltpu
from jax.sharding import PartitionSpec as P

LANES = 128
SUB = 8
FULL = 16
F32 = jnp.float32
BF16 = jnp.bfloat16
NT = (((1,), (1,)), ((), ()))
NN = (((1,), (0,)), ((), ()))


def ranks(ids, experts):
    topk, tokens = ids.shape
    expert = lax.broadcasted_iota(jnp.int32, (experts, tokens), 0)
    hit = jnp.zeros((experts, tokens), F32)
    for k in range(topk):
        hit = hit + (ids[k : k + 1, :] == expert).astype(F32)
    earlier = lax.broadcasted_iota(jnp.int32, (tokens, tokens), 0) < lax.broadcasted_iota(
        jnp.int32, (tokens, tokens), 1
    )
    before = lax.dot_general(
        hit.astype(BF16), earlier.astype(F32).astype(BF16), NN, preferred_element_type=F32
    )
    return jnp.where(hit > 0.5, before, -1.0)


def pack_kernel(
    ids_hbm, weight_hbm, cot_hbm, sent_hbm, rank_ref, ids_ref, weight_ref, cot_ref, send_ref, in_sems, out_sems
):
    inputs = [
        pltpu.make_async_copy(src, dst, in_sems.at[i])
        for i, (src, dst) in enumerate(
            ((ids_hbm, ids_ref), (weight_hbm, weight_ref), (cot_hbm, cot_ref))
        )
    ]
    for copy in inputs:
        copy.start()
    outputs = []
    experts = send_ref.shape[0]
    width, tokens = cot_ref.shape
    blocks = -(-width // LANES)
    half = blocks // 2
    whole = width // LANES * LANES
    inputs[0].wait()
    inputs[1].wait()
    ids = ids_ref[...]
    rank = ranks(ids, experts)
    rank_ref[...] = rank
    expert = lax.broadcasted_iota(jnp.int32, (experts, tokens), 0)
    gate = jnp.zeros((experts, tokens), F32)
    for k in range(ids.shape[0]):
        gate = gate + jnp.where(
            ids[k : k + 1, :] == expert, weight_ref[k : k + 1, :].astype(F32), 0.0
        )

    inputs[2].wait()
    cot = cot_ref[...]
    tail = jnp.concatenate(
        [cot[whole:], jnp.zeros((LANES - (width - whole), tokens), BF16)], axis=0
    )
    free = (
        lax.broadcasted_iota(jnp.int32, (LANES, tokens), 0) >= width - whole
    ).astype(F32).astype(BF16)

    def pick(rows, columns):
        return lax.dot_general(rows, columns, NT, preferred_element_type=F32)

    def put(first, count, value):
        send_ref[:, first : first + count, :] = value.astype(BF16).reshape(experts, count, LANES)

    def ship(first, count):
        at = (slice(None), slice(first, first + count), slice(None))
        copy = pltpu.make_async_copy(send_ref.at[at], sent_hbm.at[at], out_sems.at[len(outputs)])
        copy.start()
        outputs.append(copy)

    def select(count, wanted):
        rows = lax.broadcasted_iota(jnp.int32, (experts, count, tokens), 1)
        chosen = (rank[:, None, :] == wanted(rows).astype(F32)).astype(F32)
        gated = chosen * gate[:, None, :]
        return (
            chosen.reshape(experts * count, tokens).astype(BF16),
            gated.reshape(experts * count, tokens).astype(BF16),
        )

    rows_a, gated_a = select(FULL, lambda r: r)
    for b in range(blocks - 1):
        put(b * FULL, FULL, pick(rows_a, cot[b * LANES : (b + 1) * LANES]))
        ship(b * FULL, FULL)
    put((blocks - 1) * FULL, FULL, pick(rows_a, tail) + pick(gated_a, free))
    ship((blocks - 1) * FULL, FULL)

    base = blocks * FULL
    rows_l, _ = select(SUB, lambda r: jnp.where(r < SUB // 2, r + FULL, -2))
    rows_h, gated_h = select(SUB, lambda r: jnp.where(r < SUB // 2, -2, r + FULL - SUB // 2))
    for b in range(half):
        low = pick(rows_l, cot[b * LANES : (b + 1) * LANES])
        if half + b < blocks - 1:
            high = pick(rows_h, cot[(half + b) * LANES : (half + b + 1) * LANES])
        else:
            high = pick(rows_h, tail) + pick(gated_h, free)
        put(base + b * SUB, SUB, low + high)
        if b % 2:
            ship(base + (b - 1) * SUB, 2 * SUB)
    for copy in outputs:
        copy.wait()


def align_kernel(core_ref, act_ref, act_other_ref, weight_ref, other_low_ref, other_high_ref, out_ref):
    slots, sources, hidden = act_ref.shape
    width = weight_ref.shape[0] // 2
    blocks = -(-width // LANES)
    half = blocks // 2
    rows = out_ref.shape[0] // sources
    start = core_ref[0] * width
    acts = [ref[...].reshape(slots * sources, hidden) for ref in (act_ref, act_other_ref)]
    for first in range(0, blocks, 2):
        at, count = first * LANES, min(2 * LANES, width - first * LANES)
        out = jnp.zeros((slots * sources, 2 * LANES), F32)
        for c, act in enumerate(acts):
            if c:
                cut = other_low_ref.shape[0]
                columns = [other_low_ref[at : at + count, :]] if at < cut else []
                if at + count > cut:
                    columns.append(other_high_ref[max(at - cut, 0) : at + count - cut, :])
                columns = jnp.concatenate(columns, axis=0)
            else:
                columns = weight_ref[pl.ds(pl.multiple_of(start + at, 16), count), :]
            if count < 2 * LANES:
                columns = jnp.concatenate(
                    [columns, jnp.zeros((2 * LANES - count, hidden), BF16)], axis=0
                )
            out = out + lax.dot_general(act, columns, NT, preferred_element_type=F32)
        for b in (first, first + 1):
            for s in range(slots):
                if s < FULL:
                    row = b * FULL + s
                else:
                    row = blocks * FULL + b % half * SUB + b // half * (SUB // 2) + s - FULL
                out_ref[pl.ds(row, sources, stride=rows), :] = out[
                    s * sources : (s + 1) * sources, (b - first) * LANES : (b - first + 1) * LANES
                ]


def dots_kernel(blocks, rows_ref, aligned_hbm, dots_ref, aligned_ref, sems):
    sources = rows_ref.shape[0]
    parts = sems.shape[0]
    step = sources // parts
    copies = [
        pltpu.make_async_copy(
            aligned_hbm.at[pl.ds(p * step, step)], aligned_ref.at[pl.ds(p * step, step)], sems.at[p]
        )
        for p in range(parts)
    ]
    for copy in copies:
        copy.start()

    def reduce(p, first, count, steps):
        total = jnp.zeros((step, count, LANES), F32)
        of = slice(p * step, (p + 1) * step)
        for b in range(steps):
            at = slice(first + b * count, first + (b + 1) * count)
            total = total + rows_ref[of, at, :].astype(F32) * aligned_ref[of, at, :]
        return jnp.sum(total, axis=2, keepdims=True)

    def spread(value, count, slot):
        lane = lax.broadcasted_iota(jnp.int32, (step, count, LANES), 2)
        row = lax.broadcasted_iota(jnp.int32, (step, count, LANES), 1)
        return jnp.sum(jnp.where(lane == slot(row), value, 0.0), axis=1)

    for p in range(parts):
        copies[p].wait()
        full = spread(reduce(p, 0, FULL, blocks), FULL, lambda r: r)
        split = spread(
            reduce(p, blocks * FULL, SUB, blocks // 2),
            SUB,
            lambda r: jnp.where(r < SUB // 2, r, r - SUB // 2) + FULL,
        )
        for first in (p * step, sources + p * step):
            dots_ref[first : first + step, :] = full + split


def project_kernel(
    core_ref, own_ref, other_hbm, weight_hbm, grad_hbm, weight_ref, other_ref, grad_ref, part, tails, gates, in_sems, out_sems
):
    sources = own_ref.shape[0]
    _, width, hidden = weight_ref.shape
    slots = grad_ref.shape[0]
    columns = hidden // LANES
    blocks = -(-width // LANES)
    half = blocks // 2
    tail = width % LANES
    base = blocks * FULL
    split = sources * FULL
    mine = core_ref[0] * width

    def fetch(i, src, dst):
        copy = pltpu.make_async_copy(src, dst, in_sems.at[i])
        copy.start()
        return copy

    def weight_rows(start, count):
        return weight_hbm.at[pl.ds(pl.multiple_of(start, 16), count)]

    cut = half * LANES
    inputs = (
        fetch(0, weight_rows(mine, cut), weight_ref.at[0, :cut]),
        fetch(1, weight_rows(mine + cut, width - cut), weight_ref.at[0, cut:]),
        fetch(2, other_hbm, other_ref),
        fetch(3, weight_rows(width - mine, cut), weight_ref.at[1, :cut]),
        fetch(4, weight_rows(width - mine + cut, width - cut), weight_ref.at[1, cut:]),
    )

    def block(ref, first, count):
        return ref[:, first : first + count, :].reshape(sources * count, LANES)

    def lanes(n):
        return slice(n * LANES, (n + 1) * LANES)

    def product(ref, c, h):
        last = width - cut if h else cut

        def dot(first, count):
            rows = [block(ref, first + b * count, count) for b in range(half)]
            return lax.dot_general(
                jnp.concatenate(rows, axis=1)[:, :last],
                weight_ref[c, h * cut : h * cut + last, :],
                NN,
                preferred_element_type=F32,
            )

        return dot(h * half * FULL, FULL), dot(base, SUB)

    gates[:split] = block(own_ref, (blocks - 1) * FULL, FULL).astype(F32)
    gates[split : split + sources * SUB] = block(own_ref, base + (half - 1) * SUB, SUB).astype(F32)
    for c, ref in enumerate((own_ref, other_ref)):
        for h in (0, 1):
            if c == 1 and h == 0:
                inputs[2].wait()
            inputs[3 * c + h].wait()
            out, some = product(ref, c, h)
            for n in range(columns):
                full = out[:, lanes(n)]
                few = some[:, lanes(n)]
                if c or h:
                    full = full + part[n, :split]
                if c:
                    few = few + tails[h, n, : sources * SUB]
                part[n, :split] = full
                tails[h, n, : sources * SUB] = few

    outputs = []
    for s in range(slots):
        if s < FULL:
            gate = gates[pl.ds(s, sources, stride=FULL), :]
        else:
            gate = gates[pl.ds(split + s - FULL + SUB // 2, sources, stride=SUB), :]
        gate = jnp.broadcast_to(gate[:, tail : tail + 1], (sources, LANES))
        for n in range(columns):
            if s < FULL:
                proj = part[n, pl.ds(s, sources, stride=FULL), :]
            else:
                proj = (
                    tails[0, n, pl.ds(s - FULL, sources, stride=SUB), :]
                    + tails[1, n, pl.ds(s - FULL + SUB // 2, sources, stride=SUB), :]
                )
            grad_ref[s, :, lanes(n)] = (gate * proj).astype(BF16)
        copy = pltpu.make_async_copy(grad_ref.at[s], grad_hbm.at[s], out_sems.at[s])
        copy.start()
        outputs.append(copy)
    for copy in outputs:
        copy.wait()


def collect_kernel(slots, ids_ref, rank_ref, mine_ref, out_ref):
    experts, tokens = rank_ref.shape
    rank = rank_ref[...]
    back = mine_ref[:experts, :] + mine_ref[experts:, :]
    found = jnp.zeros((experts, tokens), F32)
    for s in range(slots):
        found = jnp.where(rank == float(s), back[:, s : s + 1], found)
    ids = ids_ref[...]
    expert = lax.broadcasted_iota(jnp.int32, (experts, tokens), 0)
    for k in range(ids.shape[0]):
        out_ref[k : k + 1, :] = jnp.sum(
            jnp.where(ids[k : k + 1, :] == expert, found, 0.0), axis=0, keepdims=True
        )


VMEM = pl.BlockSpec(memory_space=pltpu.VMEM)
HBM = pl.BlockSpec(memory_space=pltpu.HBM)
WHOLE = pltpu.CompilerParams(vmem_limit_bytes=64 * 1024 * 1024 - 128 * 1024)
MOST = pltpu.CompilerParams(vmem_limit_bytes=54 * 1000 * 1000)

PARAMS = pltpu.CompilerParams(vmem_limit_bytes=16 * 1024 * 1024)


def on_device(cotangent, route_weight, expert_ids, down_weight, hidden_act):
    experts = lax.axis_size("expert")
    tokens, width = cotangent.shape
    topk = expert_ids.shape[1]
    _, _, _, slots, hidden = hidden_act.shape
    blocks = -(-width // LANES)
    rows = blocks * FULL + blocks // 2 * SUB
    ids = expert_ids.T
    send, rank = pl.pallas_call(
        pack_kernel,
        out_shape=(
            jax.ShapeDtypeStruct((experts, rows, LANES), BF16),
            jax.ShapeDtypeStruct((experts, tokens), F32),
        ),
        in_specs=[HBM] * 3,
        out_specs=(HBM, VMEM),
        scratch_shapes=[
            pltpu.VMEM((topk, tokens), jnp.int32),
            pltpu.VMEM((topk, tokens), BF16),
            pltpu.VMEM((width, tokens), BF16),
            pltpu.VMEM((experts, rows, LANES), BF16),
            pltpu.SemaphoreType.DMA((3,)),
            pltpu.SemaphoreType.DMA((blocks + blocks // 4,)),
        ],
        compiler_params=WHOLE,
        name="pack",
    )(ids, route_weight.T, cotangent.T)
    weight, send = lax.optimization_barrier((down_weight[0].T, send))
    own = lax.all_to_all(send, "expert", split_axis=0, concat_axis=0, tiled=True)
    swap = [(0, 1), (1, 0)]
    core = lax.axis_index("fsdp").astype(jnp.int32).reshape(1)
    act = hidden_act[0, 0].swapaxes(0, 1)
    scalar = pl.BlockSpec(memory_space=pltpu.SMEM)
    act_other = lax.ppermute(act, "fsdp", swap)
    start = (1 - core[0]) * width
    cut = width // 2
    weight_other = [
        lax.ppermute(lax.dynamic_slice_in_dim(weight, start + first, cut, 0), "fsdp", swap)
        for first in (0, cut)
    ]
    both = pl.pallas_call(
        align_kernel,
        out_shape=jax.ShapeDtypeStruct((experts * rows, LANES), F32),
        in_specs=[scalar] + [VMEM] * 5,
        out_specs=VMEM,
        compiler_params=PARAMS,
        cost_estimate=pl.CostEstimate(
            flops=2 * slots * experts * weight.size, bytes_accessed=16 * 1024 * 1024, transcendentals=0
        ),
        name="align",
    )(core, act, act_other, weight, *weight_other).reshape(experts, rows, LANES)
    dots = pl.pallas_call(
        lambda *refs: dots_kernel(blocks, *refs),
        out_shape=jax.ShapeDtypeStruct((2 * experts, LANES), F32),
        in_specs=[VMEM, HBM],
        out_specs=VMEM,
        scratch_shapes=[
            pltpu.VMEM((experts, rows, LANES), F32),
            pltpu.SemaphoreType.DMA((experts // SUB,)),
        ],
        compiler_params=MOST,
        name="dots",
    )(own, both).reshape(2 * experts, 1, LANES)
    own, dots = lax.optimization_barrier((own, dots))
    back = lax.all_to_all(dots, ("fsdp", "expert"), split_axis=0, concat_axis=0, tiled=True)
    back = back.reshape(2 * experts, LANES)
    other = lax.ppermute(own, "fsdp", swap)
    grad = pl.pallas_call(
        project_kernel,
        out_shape=jax.ShapeDtypeStruct((slots, experts, hidden), BF16),
        in_specs=[scalar, VMEM, HBM, HBM],
        out_specs=HBM,
        scratch_shapes=[
            pltpu.VMEM((2, width, hidden), BF16),
            pltpu.VMEM((experts, rows, LANES), BF16),
            pltpu.VMEM((slots, experts, hidden), BF16),
            pltpu.VMEM((hidden // LANES, (experts + 1) * FULL, LANES), F32),
            pltpu.VMEM((2, hidden // LANES, (experts + 1) * SUB, LANES), F32),
            pltpu.VMEM(((experts + 1) * FULL + experts * SUB, LANES), F32),
            pltpu.SemaphoreType.DMA((5,)),
            pltpu.SemaphoreType.DMA((slots,)),
        ],
        compiler_params=MOST,
        cost_estimate=pl.CostEstimate(
            flops=2 * slots * experts * weight.size, bytes_accessed=10 * 1024 * 1024, transcendentals=0
        ),
        name="project",
    )(core, own, other, weight)
    back, grad = lax.optimization_barrier((back, grad))
    route_grad = pl.pallas_call(
        lambda *refs: collect_kernel(slots, *refs),
        out_shape=jax.ShapeDtypeStruct((topk, tokens), F32),
        in_specs=[VMEM] * 3,
        out_specs=VMEM,
        compiler_params=PARAMS,
        name="collect",
    )(ids, rank, back)
    return grad.swapaxes(0, 1)[None, None], route_grad.T


def solution(mesh):
    placed = (
        P(("dp", "expert"), "fsdp"),
        P(("dp", "expert"), None),
        P(("dp", "expert"), None),
        P("expert", "fsdp", None),
        P("dp", "expert", None, None, "fsdp"),
    )
    return jax.shard_map(
        on_device,
        mesh=mesh,
        in_specs=placed,
        out_specs=(P("dp", "expert", None, None, "fsdp"), P(("dp", "expert"), None)),
        check_vma=False,
    )
```

```python
import jax
import jax.numpy as jnp
from jax import lax
from jax.experimental import pallas as pl
from jax.experimental.pallas import tpu as pltpu
from jax.sharding import PartitionSpec as P

LANES = 128
SUB = 8
FULL = 16
F32 = jnp.float32
BF16 = jnp.bfloat16
NT = (((1,), (1,)), ((), ()))
NN = (((1,), (0,)), ((), ()))


def ranks(ids, experts):
    topk, tokens = ids.shape
    expert = lax.broadcasted_iota(jnp.int32, (experts, tokens), 0)
    hit = jnp.zeros((experts, tokens), F32)
    for k in range(topk):
        hit = hit + (ids[k : k + 1, :] == expert).astype(F32)
    earlier = lax.broadcasted_iota(jnp.int32, (tokens, tokens), 0) < lax.broadcasted_iota(
        jnp.int32, (tokens, tokens), 1
    )
    before = lax.dot_general(
        hit.astype(BF16), earlier.astype(F32).astype(BF16), NN, preferred_element_type=F32
    )
    return jnp.where(hit > 0.5, before, -1.0)


def pack_kernel(
    ids_hbm, weight_hbm, cot_hbm, sent_hbm, rank_ref, ids_ref, weight_ref, cot_ref, send_ref, in_sems, out_sems
):
    inputs = [
        pltpu.make_async_copy(src, dst, in_sems.at[i])
        for i, (src, dst) in enumerate(
            ((ids_hbm, ids_ref), (weight_hbm, weight_ref), (cot_hbm, cot_ref))
        )
    ]
    for copy in inputs:
        copy.start()
    outputs = []
    experts = send_ref.shape[0]
    width, tokens = cot_ref.shape
    blocks = -(-width // LANES)
    half = blocks // 2
    whole = width // LANES * LANES
    inputs[0].wait()
    inputs[1].wait()
    ids = ids_ref[...]
    rank = ranks(ids, experts)
    rank_ref[...] = rank
    expert = lax.broadcasted_iota(jnp.int32, (experts, tokens), 0)
    gate = jnp.zeros((experts, tokens), F32)
    for k in range(ids.shape[0]):
        gate = gate + jnp.where(
            ids[k : k + 1, :] == expert, weight_ref[k : k + 1, :].astype(F32), 0.0
        )

    inputs[2].wait()
    cot = cot_ref[...]
    extra = width - whole
    groups = LANES // extra
    lane = lax.broadcasted_iota(jnp.int32, (LANES, tokens), 0)

    def blank(count):
        return [jnp.zeros((count, tokens), BF16)] if count else []

    padded = [
        jnp.concatenate(blank(g * extra) + [cot[whole:]] + blank(LANES - (g + 1) * extra), axis=0)
        for g in range(groups)
    ]

    def pick(rows, columns):
        return lax.dot_general(rows, columns, NT, preferred_element_type=F32)

    def put(first, count, value):
        send_ref[:, first : first + count, :] = value.astype(BF16).reshape(experts, count, LANES)

    def ship(first, count):
        at = (slice(None), slice(first, first + count), slice(None))
        copy = pltpu.make_async_copy(send_ref.at[at], sent_hbm.at[at], out_sems.at[len(outputs)])
        copy.start()
        outputs.append(copy)

    def select(count, wanted):
        rows = lax.broadcasted_iota(jnp.int32, (experts, count, tokens), 1)
        chosen = (rank[:, None, :] == wanted(rows).astype(F32)).astype(F32)
        gated = chosen * gate[:, None, :]
        return (
            chosen.reshape(experts * count, tokens).astype(BF16),
            gated.reshape(experts * count, tokens).astype(BF16),
        )

    rows_a, _ = select(FULL, lambda r: r)
    for b in range(blocks - 1):
        put(b * FULL, FULL, pick(rows_a, cot[b * LANES : (b + 1) * LANES]))
        ship(b * FULL, FULL)

    base = (blocks - 1) * FULL
    quarter = SUB // 2
    rows_l, _ = select(SUB, lambda r: jnp.where(r < quarter, r + FULL, -2))
    rows_h, _ = select(SUB, lambda r: jnp.where(r < quarter, -2, r + FULL - quarter))
    for b in range(half):
        value = pick(rows_l, cot[b * LANES : (b + 1) * LANES])
        if half + b < blocks - 1:
            value += pick(rows_h, cot[(half + b) * LANES : (half + b + 1) * LANES])
        else:
            for g in range(groups):
                rows_g, _ = select(SUB, lambda r: jnp.where(r < quarter, -2, r + (g - 1) * quarter))
                value += pick(rows_g, padded[g])
        put(base + b * SUB, SUB, value)
        if b % 2:
            ship(base + (b - 1) * SUB, 2 * SUB)
    value = pick(rows_l, padded[0])
    for i in range(3):
        _, gated = select(SUB, lambda r: r + i * SUB)
        value += pick(gated, (lane == extra + i).astype(F32).astype(BF16))
    put(base + half * SUB, SUB, value)
    ship(base + half * SUB, SUB)
    for copy in outputs:
        copy.wait()


def align_kernel(core_ref, act_ref, act_other_ref, weight_ref, other_low_ref, other_high_ref, out_ref):
    slots, sources, hidden = act_ref.shape
    width = weight_ref.shape[0] // 2
    blocks = -(-width // LANES)
    half = blocks // 2
    rows = out_ref.shape[0] // sources
    start = core_ref[0] * width
    acts = [ref[...].reshape(slots * sources, hidden) for ref in (act_ref, act_other_ref)]
    whole = width // LANES * LANES
    extra = width - whole
    quarter = SUB // 2
    base = (blocks - 1) * FULL

    def columns_of(at, count):
        cut = other_low_ref.shape[0]
        other = [other_low_ref[at : at + count, :]] if at < cut else []
        if at + count > cut:
            other.append(other_high_ref[max(at - cut, 0) : at + count - cut, :])
        return (
            weight_ref[pl.ds(pl.multiple_of(start + at, 16), count), :],
            jnp.concatenate(other, axis=0),
        )

    def store(row, value):
        out_ref[pl.ds(row, sources, stride=rows), :] = value

    def slot(value, s, n=0):
        return value[s * sources : (s + 1) * sources, n * LANES : (n + 1) * LANES]

    for first in range(0, blocks - 1, 2):
        at, count = first * LANES, min(2 * LANES, whole - first * LANES)
        out = sum(
            lax.dot_general(act, columns, NT, preferred_element_type=F32)
            for act, columns in zip(acts, columns_of(at, count))
        )
        for b in range(first, first + count // LANES):
            for s in range(slots):
                if s < FULL:
                    row = b * FULL + s
                else:
                    row = base + b % half * SUB + b // half * quarter + s - FULL
                store(row, slot(out, s, b - first))

    last = columns_of(whole, extra)
    blank = jnp.zeros((extra, hidden), BF16)
    tails = []
    for g in range(LANES // extra):
        padded = [
            jnp.concatenate([x if i == g else blank for i in range(LANES // extra)], axis=0) for x in last
        ]
        tails.append(
            sum(
                lax.dot_general(
                    act[g * quarter * sources : (g + 1) * quarter * sources],
                    columns,
                    NT,
                    preferred_element_type=F32,
                )
                for act, columns in zip(acts, padded)
            )
        )
        if g == 0:
            few = sum(
                lax.dot_general(act[FULL * sources :], columns, NT, preferred_element_type=F32)
                for act, columns in zip(acts, padded)
            )
    packed = sum(tails)
    for s in range(quarter):
        store(base + (half - 1) * SUB + quarter + s, slot(packed, s))
        store(base + half * SUB + s, slot(few, s))
        store(base + half * SUB + quarter + s, jnp.zeros((sources, LANES), F32))


def dots_kernel(blocks, rows_ref, aligned_hbm, dots_ref, aligned_ref, sems):
    sources = rows_ref.shape[0]
    parts = sems.shape[0]
    step = sources // parts
    copies = [
        pltpu.make_async_copy(
            aligned_hbm.at[pl.ds(p * step, step)], aligned_ref.at[pl.ds(p * step, step)], sems.at[p]
        )
        for p in range(parts)
    ]
    for copy in copies:
        copy.start()

    quarter = SUB // 2
    half = blocks // 2
    base = (blocks - 1) * FULL
    extra = LANES // (FULL // quarter)

    def times(p, first, count):
        of, at = slice(p * step, (p + 1) * step), slice(first, first + count)
        return rows_ref[of, at, :].astype(F32) * aligned_ref[of, at, :]

    def spread(value, count, slot):
        lane = lax.broadcasted_iota(jnp.int32, (step, count, LANES), 2)
        row = lax.broadcasted_iota(jnp.int32, (step, count, LANES), 1)
        value = jnp.sum(value, axis=2, keepdims=True)
        return jnp.sum(jnp.where(lane == slot(row), value, 0.0), axis=1)

    lane = lax.broadcasted_iota(jnp.int32, (step, SUB, LANES), 2)
    row = lax.broadcasted_iota(jnp.int32, (step, SUB, LANES), 1)
    for p in range(parts):
        copies[p].wait()
        total = times(p, 0, FULL)
        for b in range(1, blocks - 1):
            total = total + times(p, b * FULL, FULL)
        dots = spread(total, FULL, lambda r: r)
        mixed = times(p, base + (half - 1) * SUB, SUB)
        total = times(p, base + half * SUB, SUB) + jnp.where(row < quarter, mixed, 0.0)
        for b in range(half - 1):
            total = total + times(p, base + b * SUB, SUB)
        dots = dots + spread(total, SUB, lambda r: jnp.where(r < quarter, r, r - quarter) + FULL)
        for g in range(FULL // quarter):
            here = (lane >= g * extra) & (lane < (g + 1) * extra)
            dots = dots + spread(
                jnp.where(here, mixed, 0.0),
                SUB,
                lambda r: jnp.where(r < quarter, -1, r + (g - 1) * quarter),
            )
        for first in (p * step, sources + p * step):
            dots_ref[first : first + step, :] = dots


def project_kernel(
    core_ref, own_ref, other_hbm, weight_hbm, grad_hbm, weight_ref, other_ref, grad_ref, part, tails, ends, gates, in_sems, out_sems
):
    sources = own_ref.shape[0]
    _, width, hidden = weight_ref.shape
    slots = grad_ref.shape[0]
    columns = hidden // LANES
    blocks = -(-width // LANES)
    half = blocks // 2
    tail = width % LANES
    base = (blocks - 1) * FULL
    quarter = SUB // 2
    few = sources * SUB
    groups = LANES // tail
    split = sources * FULL
    mine = core_ref[0] * width

    def fetch(i, src, dst):
        copy = pltpu.make_async_copy(src, dst, in_sems.at[i])
        copy.start()
        return copy

    def weight_rows(start, count):
        return weight_hbm.at[pl.ds(pl.multiple_of(start, 16), count)]

    cut = half * LANES
    inputs = (
        fetch(0, weight_rows(mine, cut), weight_ref.at[0, :cut]),
        fetch(1, weight_rows(mine + cut, width - cut), weight_ref.at[0, cut:]),
        fetch(2, other_hbm, other_ref),
        fetch(3, weight_rows(width - mine, cut), weight_ref.at[1, :cut]),
        fetch(4, weight_rows(width - mine + cut, width - cut), weight_ref.at[1, cut:]),
    )

    def block(ref, first, count):
        return ref[:, first : first + count, :].reshape(sources * count, LANES)

    def lanes(n):
        return slice(n * LANES, (n + 1) * LANES)

    def product(ref, c, h):
        steps = blocks - 1 - half if h else half

        def dot(first, count):
            rows = [block(ref, first + b * count, count) for b in range(steps)]
            return lax.dot_general(
                jnp.concatenate(rows, axis=1),
                weight_ref[c, h * cut : h * cut + steps * LANES, :],
                NN,
                preferred_element_type=F32,
            )

        return dot(h * half * FULL, FULL), dot(base, SUB)

    gates[:few] = block(own_ref, base + half * SUB, SUB).astype(F32)
    for c, ref in enumerate((own_ref, other_ref)):
        for h in (0, 1):
            if c == 1 and h == 0:
                inputs[2].wait()
            inputs[3 * c + h].wait()
            out, some = product(ref, c, h)
            for n in range(columns):
                full = out[:, lanes(n)]
                rest = some[:, lanes(n)]
                if c or h:
                    full = full + part[n, :split]
                if c:
                    rest = rest + tails[h, n, :few]
                part[n, :split] = full
                tails[h, n, :few] = rest
    lane = lax.broadcasted_iota(jnp.int32, (1, LANES), 1)
    mixed, last = [
        [block(ref, base + at * SUB, SUB) for ref in (own_ref, other_ref)] for at in (half - 1, half)
    ]
    rows = []
    for g in range(groups + 1):
        first = g % groups * tail
        keep = ((lane >= first) & (lane < first + tail)).astype(F32).astype(BF16)
        rows.append(jnp.concatenate([x * keep for x in (mixed if g < groups else last)], axis=1))
    out = lax.dot_general(
        jnp.concatenate(rows, axis=0),
        jnp.concatenate([weight_ref[c, width - tail :, :] for c in (0, 1) for _ in range(groups)], axis=0),
        NN,
        preferred_element_type=F32,
    )
    for n in range(columns):
        for g in range(groups):
            ends[g, n, :few] = out[g * few : (g + 1) * few, lanes(n)]
        tails[0, n, :few] += out[groups * few :, lanes(n)]

    outputs = []
    for s in range(slots):
        gate = gates[pl.ds(s % SUB, sources, stride=SUB), :]
        at = tail + s // SUB
        gate = jnp.broadcast_to(gate[:, at : at + 1], (sources, LANES))
        for n in range(columns):
            if s < FULL:
                proj = (
                    part[n, pl.ds(s, sources, stride=FULL), :]
                    + ends[s // quarter, n, pl.ds(quarter + s % quarter, sources, stride=SUB), :]
                )
            else:
                proj = (
                    tails[0, n, pl.ds(s - FULL, sources, stride=SUB), :]
                    + tails[1, n, pl.ds(s - FULL + SUB // 2, sources, stride=SUB), :]
                )
            grad_ref[s, :, lanes(n)] = (gate * proj).astype(BF16)
        copy = pltpu.make_async_copy(grad_ref.at[s], grad_hbm.at[s], out_sems.at[s])
        copy.start()
        outputs.append(copy)
    for copy in outputs:
        copy.wait()


def collect_kernel(slots, ids_ref, rank_ref, mine_ref, out_ref):
    experts, tokens = rank_ref.shape
    rank = rank_ref[...]
    back = mine_ref[:experts, :] + mine_ref[experts:, :]
    found = jnp.zeros((experts, tokens), F32)
    for s in range(slots):
        found = jnp.where(rank == float(s), back[:, s : s + 1], found)
    ids = ids_ref[...]
    expert = lax.broadcasted_iota(jnp.int32, (experts, tokens), 0)
    for k in range(ids.shape[0]):
        out_ref[k : k + 1, :] = jnp.sum(
            jnp.where(ids[k : k + 1, :] == expert, found, 0.0), axis=0, keepdims=True
        )


VMEM = pl.BlockSpec(memory_space=pltpu.VMEM)
HBM = pl.BlockSpec(memory_space=pltpu.HBM)
WHOLE = pltpu.CompilerParams(vmem_limit_bytes=64 * 1024 * 1024 - 128 * 1024)
MOST = pltpu.CompilerParams(vmem_limit_bytes=54 * 1000 * 1000)

PARAMS = pltpu.CompilerParams(vmem_limit_bytes=16 * 1024 * 1024)


def on_device(cotangent, route_weight, expert_ids, down_weight, hidden_act):
    experts = lax.axis_size("expert")
    tokens, width = cotangent.shape
    topk = expert_ids.shape[1]
    _, _, _, slots, hidden = hidden_act.shape
    blocks = -(-width // LANES)
    rows = (blocks - 1) * FULL + (blocks // 2 + 1) * SUB
    ids = expert_ids.T
    send, rank = pl.pallas_call(
        pack_kernel,
        out_shape=(
            jax.ShapeDtypeStruct((experts, rows, LANES), BF16),
            jax.ShapeDtypeStruct((experts, tokens), F32),
        ),
        in_specs=[HBM] * 3,
        out_specs=(HBM, VMEM),
        scratch_shapes=[
            pltpu.VMEM((topk, tokens), jnp.int32),
            pltpu.VMEM((topk, tokens), BF16),
            pltpu.VMEM((width, tokens), BF16),
            pltpu.VMEM((experts, rows, LANES), BF16),
            pltpu.SemaphoreType.DMA((3,)),
            pltpu.SemaphoreType.DMA((blocks + blocks // 4,)),
        ],
        compiler_params=WHOLE,
        name="pack",
    )(ids, route_weight.T, cotangent.T)
    weight, send = lax.optimization_barrier((down_weight[0].T, send))
    own = lax.all_to_all(send, "expert", split_axis=0, concat_axis=0, tiled=True)
    swap = [(0, 1), (1, 0)]
    core = lax.axis_index("fsdp").astype(jnp.int32).reshape(1)
    act = hidden_act[0, 0].swapaxes(0, 1)
    scalar = pl.BlockSpec(memory_space=pltpu.SMEM)
    act_other = lax.ppermute(act, "fsdp", swap)
    start = (1 - core[0]) * width
    cut = width // 2
    weight_other = [
        lax.ppermute(lax.dynamic_slice_in_dim(weight, start + first, cut, 0), "fsdp", swap)
        for first in (0, cut)
    ]
    both = pl.pallas_call(
        align_kernel,
        out_shape=jax.ShapeDtypeStruct((experts * rows, LANES), F32),
        in_specs=[scalar] + [VMEM] * 5,
        out_specs=VMEM,
        compiler_params=PARAMS,
        cost_estimate=pl.CostEstimate(
            flops=2 * slots * experts * weight.size, bytes_accessed=16 * 1024 * 1024, transcendentals=0
        ),
        name="align",
    )(core, act, act_other, weight, *weight_other).reshape(experts, rows, LANES)
    dots = pl.pallas_call(
        lambda *refs: dots_kernel(blocks, *refs),
        out_shape=jax.ShapeDtypeStruct((2 * experts, LANES), F32),
        in_specs=[VMEM, HBM],
        out_specs=VMEM,
        scratch_shapes=[
            pltpu.VMEM((experts, rows, LANES), F32),
            pltpu.SemaphoreType.DMA((experts // SUB,)),
        ],
        compiler_params=MOST,
        name="dots",
    )(own, both).reshape(2 * experts, 1, LANES)
    own, dots = lax.optimization_barrier((own, dots))
    back = lax.all_to_all(dots, ("fsdp", "expert"), split_axis=0, concat_axis=0, tiled=True)
    back = back.reshape(2 * experts, LANES)
    other = lax.ppermute(own, "fsdp", swap)
    grad = pl.pallas_call(
        project_kernel,
        out_shape=jax.ShapeDtypeStruct((slots, experts, hidden), BF16),
        in_specs=[scalar, VMEM, HBM, HBM],
        out_specs=HBM,
        scratch_shapes=[
            pltpu.VMEM((2, width, hidden), BF16),
            pltpu.VMEM((experts, rows, LANES), BF16),
            pltpu.VMEM((slots, experts, hidden), BF16),
            pltpu.VMEM((hidden // LANES, (experts + 1) * FULL, LANES), F32),
            pltpu.VMEM((2, hidden // LANES, (experts + 1) * SUB, LANES), F32),
            pltpu.VMEM((LANES // (width % LANES), hidden // LANES, (experts + 1) * SUB, LANES), F32),
            pltpu.VMEM(((experts + 1) * SUB, LANES), F32),
            pltpu.SemaphoreType.DMA((5,)),
            pltpu.SemaphoreType.DMA((slots,)),
        ],
        compiler_params=MOST,
        cost_estimate=pl.CostEstimate(
            flops=2 * slots * experts * weight.size, bytes_accessed=10 * 1024 * 1024, transcendentals=0
        ),
        name="project",
    )(core, own, other, weight)
    back, grad = lax.optimization_barrier((back, grad))
    route_grad = pl.pallas_call(
        lambda *refs: collect_kernel(slots, *refs),
        out_shape=jax.ShapeDtypeStruct((topk, tokens), F32),
        in_specs=[VMEM] * 3,
        out_specs=VMEM,
        compiler_params=PARAMS,
        name="collect",
    )(ids, rank, back)
    return grad.swapaxes(0, 1)[None, None], route_grad.T


def solution(mesh):
    placed = (
        P(("dp", "expert"), "fsdp"),
        P(("dp", "expert"), None),
        P(("dp", "expert"), None),
        P("expert", "fsdp", None),
        P("dp", "expert", None, None, "fsdp"),
    )
    return jax.shard_map(
        on_device,
        mesh=mesh,
        in_specs=placed,
        out_specs=(P("dp", "expert", None, None, "fsdp"), P(("dp", "expert"), None)),
        check_vma=False,
    )
```

```python
import jax
import jax.numpy as jnp
from jax import lax
from jax.experimental import pallas as pl
from jax.experimental.pallas import tpu as pltpu
from jax.sharding import PartitionSpec as P

LANES = 128
SUB = 8
FULL = 16
F32 = jnp.float32
BF16 = jnp.bfloat16
NT = (((1,), (1,)), ((), ()))
NN = (((1,), (0,)), ((), ()))


def ranks(ids, experts):
    topk, tokens = ids.shape
    expert = lax.broadcasted_iota(jnp.int32, (experts, tokens), 0)
    hit = jnp.zeros((experts, tokens), F32)
    for k in range(topk):
        hit = hit + (ids[k : k + 1, :] == expert).astype(F32)
    earlier = lax.broadcasted_iota(jnp.int32, (tokens, tokens), 0) < lax.broadcasted_iota(
        jnp.int32, (tokens, tokens), 1
    )
    before = lax.dot_general(
        hit.astype(BF16), earlier.astype(F32).astype(BF16), NN, preferred_element_type=F32
    )
    return jnp.where(hit > 0.5, before, -1.0)


def pack_kernel(
    ids_hbm, weight_hbm, cot_hbm, sent_hbm, rank_ref, ids_ref, weight_ref, cot_ref, send_ref, in_sems, out_sems
):
    inputs = [
        pltpu.make_async_copy(src, dst, in_sems.at[i])
        for i, (src, dst) in enumerate(
            ((ids_hbm, ids_ref), (weight_hbm, weight_ref), (cot_hbm, cot_ref))
        )
    ]
    for copy in inputs:
        copy.start()
    outputs = []
    experts = send_ref.shape[0]
    width, tokens = cot_ref.shape
    blocks = -(-width // LANES)
    half = blocks // 2
    whole = width // LANES * LANES
    inputs[0].wait()
    inputs[1].wait()
    ids = ids_ref[...]
    rank = ranks(ids, experts)
    rank_ref[...] = rank
    expert = lax.broadcasted_iota(jnp.int32, (experts, tokens), 0)
    gate = jnp.zeros((experts, tokens), F32)
    for k in range(ids.shape[0]):
        gate = gate + jnp.where(
            ids[k : k + 1, :] == expert, weight_ref[k : k + 1, :].astype(F32), 0.0
        )

    inputs[2].wait()
    cot = cot_ref[...]
    extra = width - whole
    groups = LANES // extra
    lane = lax.broadcasted_iota(jnp.int32, (LANES, tokens), 0)

    def blank(count):
        return [jnp.zeros((count, tokens), BF16)] if count else []

    padded = [
        jnp.concatenate(blank(g * extra) + [cot[whole:]] + blank(LANES - (g + 1) * extra), axis=0)
        for g in range(groups)
    ]

    def pick(rows, columns):
        return lax.dot_general(rows, columns, NT, preferred_element_type=F32)

    def put(first, count, value):
        send_ref[:, first : first + count, :] = value.astype(BF16).reshape(experts, count, LANES)

    def ship(first, count):
        at = (slice(None), slice(first, first + count), slice(None))
        copy = pltpu.make_async_copy(send_ref.at[at], sent_hbm.at[at], out_sems.at[len(outputs)])
        copy.start()
        outputs.append(copy)

    def select(count, wanted):
        rows = lax.broadcasted_iota(jnp.int32, (experts, count, tokens), 1)
        chosen = (rank[:, None, :] == wanted(rows).astype(F32)).astype(F32)
        gated = chosen * gate[:, None, :]
        return (
            chosen.reshape(experts * count, tokens).astype(BF16),
            gated.reshape(experts * count, tokens).astype(BF16),
        )

    rows_a, _ = select(FULL, lambda r: r)
    for b in range(blocks - 1):
        put(b * FULL, FULL, pick(rows_a, cot[b * LANES : (b + 1) * LANES]))
        ship(b * FULL, FULL)

    base = (blocks - 1) * FULL
    quarter = SUB // 2
    rows_l, _ = select(SUB, lambda r: jnp.where(r < quarter, r + FULL, -2))
    rows_h, _ = select(SUB, lambda r: jnp.where(r < quarter, -2, r + FULL - quarter))
    for b in range(half):
        value = pick(rows_l, cot[b * LANES : (b + 1) * LANES])
        if half + b < blocks - 1:
            value += pick(rows_h, cot[(half + b) * LANES : (half + b + 1) * LANES])
        else:
            for g in range(groups):
                rows_g, _ = select(SUB, lambda r: jnp.where(r < quarter, -2, r + (g - 1) * quarter))
                value += pick(rows_g, padded[g])
        put(base + b * SUB, SUB, value)
        if b % 2:
            ship(base + (b - 1) * SUB, 2 * SUB)
    value = pick(rows_l, padded[0])
    for i in range(3):
        _, gated = select(SUB, lambda r: r + i * SUB)
        value += pick(gated, (lane == extra + i).astype(F32).astype(BF16))
    put(base + half * SUB, SUB, value)
    ship(base + half * SUB, SUB)
    for copy in outputs:
        copy.wait()


def align_kernel(core_ref, act_ref, act_other_ref, weight_ref, other_low_ref, other_high_ref, out_ref):
    slots, sources, hidden = act_ref.shape
    width = weight_ref.shape[0] // 2
    blocks = -(-width // LANES)
    half = blocks // 2
    rows = out_ref.shape[0] // sources
    start = core_ref[0] * width
    acts = [ref[...].reshape(slots * sources, hidden) for ref in (act_ref, act_other_ref)]
    whole = width // LANES * LANES
    extra = width - whole
    quarter = SUB // 2
    base = (blocks - 1) * FULL

    def columns_of(at, count):
        cut = other_low_ref.shape[0]
        other = [other_low_ref[at : at + count, :]] if at < cut else []
        if at + count > cut:
            other.append(other_high_ref[max(at - cut, 0) : at + count - cut, :])
        return (
            weight_ref[pl.ds(pl.multiple_of(start + at, 16), count), :],
            jnp.concatenate(other, axis=0),
        )

    def store(row, value):
        out_ref[pl.ds(row, sources, stride=rows), :] = value

    def slot(value, s, n=0):
        return value[s * sources : (s + 1) * sources, n * LANES : (n + 1) * LANES]

    for first in range(0, blocks - 1, 2):
        at, count = first * LANES, min(2 * LANES, whole - first * LANES)
        out = sum(
            lax.dot_general(act, columns, NT, preferred_element_type=F32)
            for act, columns in zip(acts, columns_of(at, count))
        )
        for b in range(first, first + count // LANES):
            for s in range(slots):
                if s < FULL:
                    row = b * FULL + s
                else:
                    row = base + b % half * SUB + b // half * quarter + s - FULL
                store(row, slot(out, s, b - first))

    last = columns_of(whole, extra)
    blank = jnp.zeros((extra, hidden), BF16)
    tails = []
    for g in range(LANES // extra):
        padded = [
            jnp.concatenate([x if i == g else blank for i in range(LANES // extra)], axis=0) for x in last
        ]
        tails.append(
            sum(
                lax.dot_general(
                    act[g * quarter * sources : (g + 1) * quarter * sources],
                    columns,
                    NT,
                    preferred_element_type=F32,
                )
                for act, columns in zip(acts, padded)
            )
        )
        if g == 0:
            few = sum(
                lax.dot_general(act[FULL * sources :], columns, NT, preferred_element_type=F32)
                for act, columns in zip(acts, padded)
            )
    packed = sum(tails)
    for s in range(quarter):
        store(base + (half - 1) * SUB + quarter + s, slot(packed, s))
        store(base + half * SUB + s, slot(few, s))
        store(base + half * SUB + quarter + s, jnp.zeros((sources, LANES), F32))


def dots_kernel(blocks, rows_ref, aligned_hbm, dots_ref, aligned_ref, sems):
    sources = rows_ref.shape[0]
    parts = sems.shape[0]
    step = sources // parts
    copies = [
        pltpu.make_async_copy(
            aligned_hbm.at[pl.ds(p * step, step)], aligned_ref.at[pl.ds(p * step, step)], sems.at[p]
        )
        for p in range(parts)
    ]
    for copy in copies:
        copy.start()

    quarter = SUB // 2
    half = blocks // 2
    base = (blocks - 1) * FULL
    extra = LANES // (FULL // quarter)

    def times(p, first, count):
        of, at = slice(p * step, (p + 1) * step), slice(first, first + count)
        return rows_ref[of, at, :].astype(F32) * aligned_ref[of, at, :]

    def spread(value, count, slot):
        lane = lax.broadcasted_iota(jnp.int32, (step, count, LANES), 2)
        row = lax.broadcasted_iota(jnp.int32, (step, count, LANES), 1)
        value = jnp.sum(value, axis=2, keepdims=True)
        return jnp.sum(jnp.where(lane == slot(row), value, 0.0), axis=1)

    lane = lax.broadcasted_iota(jnp.int32, (step, SUB, LANES), 2)
    row = lax.broadcasted_iota(jnp.int32, (step, SUB, LANES), 1)
    for p in range(parts):
        copies[p].wait()
        total = times(p, 0, FULL)
        for b in range(1, blocks - 1):
            total = total + times(p, b * FULL, FULL)
        dots = spread(total, FULL, lambda r: r)
        mixed = times(p, base + (half - 1) * SUB, SUB)
        total = times(p, base + half * SUB, SUB) + jnp.where(row < quarter, mixed, 0.0)
        for b in range(half - 1):
            total = total + times(p, base + b * SUB, SUB)
        dots = dots + spread(total, SUB, lambda r: jnp.where(r < quarter, r, r - quarter) + FULL)
        for g in range(FULL // quarter):
            here = (lane >= g * extra) & (lane < (g + 1) * extra)
            dots = dots + spread(
                jnp.where(here, mixed, 0.0),
                SUB,
                lambda r: jnp.where(r < quarter, -1, r + (g - 1) * quarter),
            )
        for core in (0, 1):
            dots_ref[pl.ds(2 * p * step + core, step, stride=2), :] = dots


def project_kernel(
    core_ref, own_ref, other_hbm, weight_hbm, grad_hbm, weight_ref, other_ref, grad_ref, part, tails, ends, gates, in_sems, out_sems
):
    sources = own_ref.shape[0]
    _, width, hidden = weight_ref.shape
    slots = grad_ref.shape[0]
    columns = hidden // LANES
    blocks = -(-width // LANES)
    half = blocks // 2
    tail = width % LANES
    base = (blocks - 1) * FULL
    quarter = SUB // 2
    few = sources * SUB
    groups = LANES // tail
    split = sources * FULL
    mine = core_ref[0] * width

    def fetch(i, src, dst):
        copy = pltpu.make_async_copy(src, dst, in_sems.at[i])
        copy.start()
        return copy

    def weight_rows(start, count):
        return weight_hbm.at[pl.ds(pl.multiple_of(start, 16), count)]

    cut = half * LANES
    inputs = (
        fetch(0, weight_rows(mine, cut), weight_ref.at[0, :cut]),
        fetch(1, weight_rows(mine + cut, width - cut), weight_ref.at[0, cut:]),
        fetch(2, other_hbm, other_ref),
        fetch(3, weight_rows(width - mine, cut), weight_ref.at[1, :cut]),
        fetch(4, weight_rows(width - mine + cut, width - cut), weight_ref.at[1, cut:]),
    )

    def block(ref, first, count):
        return ref[:, first : first + count, :].reshape(sources * count, LANES)

    def lanes(n):
        return slice(n * LANES, (n + 1) * LANES)

    def product(ref, c, h):
        steps = blocks - 1 - half if h else half

        def dot(first, count):
            rows = [block(ref, first + b * count, count) for b in range(steps)]
            return lax.dot_general(
                jnp.concatenate(rows, axis=1),
                weight_ref[c, h * cut : h * cut + steps * LANES, :],
                NN,
                preferred_element_type=F32,
            )

        return dot(h * half * FULL, FULL), dot(base, SUB)

    gates[:few] = block(own_ref, base + half * SUB, SUB).astype(F32)
    for c, ref in enumerate((own_ref, other_ref)):
        for h in (0, 1):
            if c == 1 and h == 0:
                inputs[2].wait()
            inputs[3 * c + h].wait()
            out, some = product(ref, c, h)
            for n in range(columns):
                full = out[:, lanes(n)]
                rest = some[:, lanes(n)]
                if c or h:
                    full = full + part[n, :split]
                if c:
                    rest = rest + tails[h, n, :few]
                part[n, :split] = full
                tails[h, n, :few] = rest
    lane = lax.broadcasted_iota(jnp.int32, (1, LANES), 1)
    mixed, last = [
        [block(ref, base + at * SUB, SUB) for ref in (own_ref, other_ref)] for at in (half - 1, half)
    ]
    rows = []
    for g in range(groups + 1):
        first = g % groups * tail
        keep = ((lane >= first) & (lane < first + tail)).astype(F32).astype(BF16)
        rows.append(jnp.concatenate([x * keep for x in (mixed if g < groups else last)], axis=1))
    out = lax.dot_general(
        jnp.concatenate(rows, axis=0),
        jnp.concatenate([weight_ref[c, width - tail :, :] for c in (0, 1) for _ in range(groups)], axis=0),
        NN,
        preferred_element_type=F32,
    )
    for n in range(columns):
        for g in range(groups):
            ends[g, n, :few] = out[g * few : (g + 1) * few, lanes(n)]
        tails[0, n, :few] += out[groups * few :, lanes(n)]

    outputs = []
    for s in range(slots):
        gate = gates[pl.ds(s % SUB, sources, stride=SUB), :]
        at = tail + s // SUB
        gate = jnp.broadcast_to(gate[:, at : at + 1], (sources, LANES))
        for n in range(columns):
            if s < FULL:
                proj = (
                    part[n, pl.ds(s, sources, stride=FULL), :]
                    + ends[s // quarter, n, pl.ds(quarter + s % quarter, sources, stride=SUB), :]
                )
            else:
                proj = (
                    tails[0, n, pl.ds(s - FULL, sources, stride=SUB), :]
                    + tails[1, n, pl.ds(s - FULL + SUB // 2, sources, stride=SUB), :]
                )
            grad_ref[s, :, lanes(n)] = (gate * proj).astype(BF16)
        copy = pltpu.make_async_copy(grad_ref.at[s], grad_hbm.at[s], out_sems.at[s])
        copy.start()
        outputs.append(copy)
    for copy in outputs:
        copy.wait()


def collect_kernel(slots, ids_ref, rank_ref, mine_ref, out_ref):
    experts, tokens = rank_ref.shape
    rank = rank_ref[...]
    back = mine_ref[pl.ds(0, experts, stride=2), :] + mine_ref[pl.ds(1, experts, stride=2), :]
    found = jnp.zeros((experts, tokens), F32)
    for s in range(slots):
        found = jnp.where(rank == float(s), back[:, s : s + 1], found)
    ids = ids_ref[...]
    expert = lax.broadcasted_iota(jnp.int32, (experts, tokens), 0)
    for k in range(ids.shape[0]):
        out_ref[k : k + 1, :] = jnp.sum(
            jnp.where(ids[k : k + 1, :] == expert, found, 0.0), axis=0, keepdims=True
        )


VMEM = pl.BlockSpec(memory_space=pltpu.VMEM)
HBM = pl.BlockSpec(memory_space=pltpu.HBM)
WHOLE = pltpu.CompilerParams(vmem_limit_bytes=64 * 1024 * 1024 - 128 * 1024)
MOST = pltpu.CompilerParams(vmem_limit_bytes=54 * 1000 * 1000)

PARAMS = pltpu.CompilerParams(vmem_limit_bytes=16 * 1024 * 1024)


def on_device(cotangent, route_weight, expert_ids, down_weight, hidden_act):
    experts = lax.axis_size("expert")
    tokens, width = cotangent.shape
    topk = expert_ids.shape[1]
    _, _, _, slots, hidden = hidden_act.shape
    blocks = -(-width // LANES)
    rows = (blocks - 1) * FULL + (blocks // 2 + 1) * SUB
    ids = expert_ids.T
    send, rank = pl.pallas_call(
        pack_kernel,
        out_shape=(
            jax.ShapeDtypeStruct((experts, rows, LANES), BF16),
            jax.ShapeDtypeStruct((experts, tokens), F32),
        ),
        in_specs=[HBM] * 3,
        out_specs=(HBM, VMEM),
        scratch_shapes=[
            pltpu.VMEM((topk, tokens), jnp.int32),
            pltpu.VMEM((topk, tokens), BF16),
            pltpu.VMEM((width, tokens), BF16),
            pltpu.VMEM((experts, rows, LANES), BF16),
            pltpu.SemaphoreType.DMA((3,)),
            pltpu.SemaphoreType.DMA((blocks + blocks // 4,)),
        ],
        compiler_params=WHOLE,
        name="pack",
    )(ids, route_weight.T, cotangent.T)
    weight, send = lax.optimization_barrier((down_weight[0].T, send))
    own = lax.all_to_all(send, "expert", split_axis=0, concat_axis=0, tiled=True)
    swap = [(0, 1), (1, 0)]
    core = lax.axis_index("fsdp").astype(jnp.int32).reshape(1)
    act = hidden_act[0, 0].swapaxes(0, 1)
    scalar = pl.BlockSpec(memory_space=pltpu.SMEM)
    act_other = lax.ppermute(act, "fsdp", swap)
    start = (1 - core[0]) * width
    cut = width // 2
    weight_other = [
        lax.ppermute(lax.dynamic_slice_in_dim(weight, start + first, cut, 0), "fsdp", swap)
        for first in (0, cut)
    ]
    both = pl.pallas_call(
        align_kernel,
        out_shape=jax.ShapeDtypeStruct((experts * rows, LANES), F32),
        in_specs=[scalar] + [VMEM] * 5,
        out_specs=VMEM,
        compiler_params=PARAMS,
        cost_estimate=pl.CostEstimate(
            flops=2 * slots * experts * weight.size, bytes_accessed=16 * 1024 * 1024, transcendentals=0
        ),
        name="align",
    )(core, act, act_other, weight, *weight_other).reshape(experts, rows, LANES)
    dots = pl.pallas_call(
        lambda *refs: dots_kernel(blocks, *refs),
        out_shape=jax.ShapeDtypeStruct((2 * experts, LANES), F32),
        in_specs=[VMEM, HBM],
        out_specs=VMEM,
        scratch_shapes=[
            pltpu.VMEM((experts, rows, LANES), F32),
            pltpu.SemaphoreType.DMA((experts // SUB,)),
        ],
        compiler_params=MOST,
        name="dots",
    )(own, both).reshape(2 * experts, 1, LANES)
    own, dots = lax.optimization_barrier((own, dots))
    back = lax.all_to_all(dots, ("expert", "fsdp"), split_axis=0, concat_axis=0, tiled=True)
    back = back.reshape(2 * experts, LANES)
    other = lax.ppermute(own, "fsdp", swap)
    grad = pl.pallas_call(
        project_kernel,
        out_shape=jax.ShapeDtypeStruct((slots, experts, hidden), BF16),
        in_specs=[scalar, VMEM, HBM, HBM],
        out_specs=HBM,
        scratch_shapes=[
            pltpu.VMEM((2, width, hidden), BF16),
            pltpu.VMEM((experts, rows, LANES), BF16),
            pltpu.VMEM((slots, experts, hidden), BF16),
            pltpu.VMEM((hidden // LANES, (experts + 1) * FULL, LANES), F32),
            pltpu.VMEM((2, hidden // LANES, (experts + 1) * SUB, LANES), F32),
            pltpu.VMEM((LANES // (width % LANES), hidden // LANES, (experts + 1) * SUB, LANES), F32),
            pltpu.VMEM(((experts + 1) * SUB, LANES), F32),
            pltpu.SemaphoreType.DMA((5,)),
            pltpu.SemaphoreType.DMA((slots,)),
        ],
        compiler_params=MOST,
        cost_estimate=pl.CostEstimate(
            flops=2 * slots * experts * weight.size, bytes_accessed=10 * 1024 * 1024, transcendentals=0
        ),
        name="project",
    )(core, own, other, weight)
    back, grad = lax.optimization_barrier((back, grad))
    route_grad = pl.pallas_call(
        lambda *refs: collect_kernel(slots, *refs),
        out_shape=jax.ShapeDtypeStruct((topk, tokens), F32),
        in_specs=[VMEM] * 3,
        out_specs=VMEM,
        compiler_params=PARAMS,
        name="collect",
    )(ids, rank, back)
    return grad.swapaxes(0, 1)[None, None], route_grad.T


def solution(mesh):
    placed = (
        P(("dp", "expert"), "fsdp"),
        P(("dp", "expert"), None),
        P(("dp", "expert"), None),
        P("expert", "fsdp", None),
        P("dp", "expert", None, None, "fsdp"),
    )
    return jax.shard_map(
        on_device,
        mesh=mesh,
        in_specs=placed,
        out_specs=(P("dp", "expert", None, None, "fsdp"), P(("dp", "expert"), None)),
        check_vma=False,
    )
```
